256 devices in a mesh: along: 16 (over y, x), cross: 8 (over z), depth: 2 (over core).
Axes of the slice: x: 4, y: 4, z: 8, core: 2. Of those that a mesh axis runs over, the one named last changes fastest.
Arguments:
- offsets: float32 [3, 64, 32, 4, 128], P(None, 'along', 'cross', 'depth'), may hold values from 0 to 1
- velocity: float32 [3, 64, 32, 4, 128], P(None, 'along', 'cross', 'depth'), may hold values from -3 to 3
- density: float32 [64, 32, 4, 128], P('along', 'cross', 'depth'), may hold values from 0.97 to 1.03
- mass: float32 [64, 32, 4, 128], P('along', 'cross', 'depth'), may hold values from 0.004 to 0.012
- pairs: int32 [26, 64, 32, 4], P(None, 'along', 'cross', 'depth'), may hold values from 0 to 1, as said below
Outputs:
- rates: float32 [4, 64, 32, 4, 128], P(None, 'along', 'cross', 'depth')
- advanced: float32 [7, 64, 32, 4, 128], P(None, 'along', 'cross', 'depth')
The draws below stay inside these ranges and needn't reach their ends.
Inputs may be any that keep to these rules, and one draw needn't show every extreme that they name: A flag marks a tile that may hold pairs within reach: the particles of each block lie in a box inside its cell, and the flag is 1 exactly when the boxes of the two blocks, placed at their grid positions, are less than 1 apart. The flags are symmetric: pairs[k] at block b equals pairs[25 - k] at the block b + (offset k); a flag whose neighbour block lies outside the grid of 64 x 32 x 4 blocks is 0.
All inputs are finite; a program needn't handle non-finite values.
Results may differ from the reference program's by a relative error of at most 0.0001.
Values sent between devices are 32-bit elements; how exact they have to be, the bound alone decides.
A program may use at most 64 MiB of HBM per device.

```python
import math
import jax
import jax.numpy as jnp
from jax import lax

BLOCK = 128
BA = 4
BC = 4
BD = 2
GA = 64
GC = 32
GD = 4


def block_boxes(key):
    level_key, extent_key, lower_key = jax.random.split(jax.random.fold_in(key, 11), 3)
    levels = jax.random.randint(level_key, (GA // BA, GC // BC, GD // BD), 1, 9)
    level_grid = jnp.repeat(jnp.repeat(jnp.repeat(levels, BA, axis=0), BC, axis=1), BD, axis=2)
    jitter = jax.random.randint(extent_key, (3, GA, GC, GD), -1, 2)
    extent = jnp.clip(level_grid[None] + jitter, 1, 8)
    lower = jax.random.randint(lower_key, (3, GA, GC, GD), 0, 9 - extent)
    return (lower, lower + extent)


def draw_offsets(key, part):
    lower, upper = block_boxes(key)
    key = jax.random.fold_in(key, 7)
    unit = jax.random.uniform(key, (3, GA, GC, GD, BLOCK), jnp.float32)
    low_f = lower.astype(jnp.float32)[..., None] / 8.0
    width_f = (upper - lower).astype(jnp.float32)[..., None] / 8.0
    return low_f + unit * width_f


def draw_pairs(key, part):
    lower, upper = block_boxes(key)
    along_pos = lax.broadcasted_iota(jnp.int32, (GA, GC, GD), 0)
    cross_pos = lax.broadcasted_iota(jnp.int32, (GA, GC, GD), 1)
    depth_pos = lax.broadcasted_iota(jnp.int32, (GA, GC, GD), 2)
    low_pad = jnp.pad(lower, ((0, 0), (1, 1), (1, 1), (1, 1)))
    high_pad = jnp.pad(upper, ((0, 0), (1, 1), (1, 1), (1, 1)))
    flags = []
    for offset_id in range(27):
        if offset_id == 13:
            continue
        steps = (offset_id // 9 - 1, offset_id // 3 % 3 - 1, offset_id % 3 - 1)
        low_n = low_pad[:, 1 + steps[0]:1 + steps[0] + GA, 1 + steps[1]:1 + steps[1] + GC, 1 + steps[2]:1 + steps[2] + GD]
        high_n = high_pad[:, 1 + steps[0]:1 + steps[0] + GA, 1 + steps[1]:1 + steps[1] + GC, 1 + steps[2]:1 + steps[2] + GD]
        total = jnp.zeros((GA, GC, GD), jnp.int32)
        for component in range(3):
            gap = jnp.maximum(8 * steps[component] + low_n[component] - upper[component], lower[component] - 8 * steps[component] - high_n[component])
            gap = jnp.maximum(gap, 0)
            total = total + gap * gap
        inside = (along_pos + steps[0] >= 0) & (along_pos + steps[0] < GA)
        inside = inside & (cross_pos + steps[1] >= 0) & (cross_pos + steps[1] < GC)
        inside = inside & (depth_pos + steps[2] >= 0) & (depth_pos + steps[2] < GD)
        flags.append(((total < 64) & inside).astype(jnp.int32))
    return jnp.stack(flags).astype(jnp.int32)


def block_scale(rng, shape, shards, low, top_value):
    def one(position, shards_of):
        heights = jax.random.uniform(jax.random.fold_in(jax.random.fold_in(rng, 6), position), (shards_of,), jnp.float32, low / len(shards), top_value / len(shards))
        return jnp.repeat(jnp.exp(heights), shape[position] // shards_of).reshape((-1,) + (1,) * (len(shape) - position - 1))

    level = one(*shards[0])
    for cut in shards[1:]:
        level = level * one(*cut)
    return level


def scatter_about(rng, shape, deviation, limit, pieces=(), dtype=jnp.bfloat16):
    values = jax.random.normal(rng, shape, jnp.float32) * deviation
    if len(pieces) > 0:
        values = block_scale(rng, shape, pieces, -0.22, 0.18) * values
    return jnp.clip(values, min=-limit, max=limit).astype(dtype)


def setup_inputs(seed: int = 0) -> dict:
    seeds = jax.random.split(jax.random.key(seed), 6)
    offsets = draw_offsets(jax.random.fold_in(seeds[5], 71), 0)
    velocity = scatter_about(seeds[1], (3, GA, GC, GD, BLOCK), 0.5, 3.0, ((1, 16), (2, 8), (3, 2)), jnp.float32)
    density = jnp.clip(0.97 + 0.059999943 * jax.random.uniform(seeds[2], (GA, GC, GD, BLOCK), jnp.float32) ** block_scale(seeds[2], (GA, GC, GD, BLOCK), ((0, 16), (1, 8), (2, 2)), -0.2, 0.2), 0.97, 1.03)
    mass = jnp.clip(jnp.exp(math.log(0.012) - 1.09861225 * jax.random.uniform(seeds[3], (GA, GC, GD, BLOCK), jnp.float32) ** block_scale(seeds[3], (GA, GC, GD, BLOCK), ((0, 16), (1, 8), (2, 2)), -0.2, 0.2)), 0.004, 0.012)
    pairs = draw_pairs(jax.random.fold_in(seeds[5], 71), 0)
    return dict(offsets=offsets, velocity=velocity, density=density, mass=mass, pairs=pairs)


SMOOTH = 0.5
SOUND_SPEED = 10.0
ARTIFICIAL = 0.5
TIME_STEP = 0.01
STIFFNESS = SOUND_SPEED * SOUND_SPEED / 7.0
KERNEL = 105.0 / (16.0 * math.pi * SMOOTH ** 5)
GRAVITY = (0.0, 0.35, 0.0, -0.94)

def pressure_term(dens_value):
    return STIFFNESS * (dens_value ** 7 - 1.0) / (dens_value * dens_value)

def pair_terms(left_block, right_block, shift_vec):
    separation = [left_block[..., component, :, None] - right_block[..., component, None, :] - shift_vec[..., component, None, None] for component in range(3)]
    relative = [left_block[..., 3 + component, :, None] - right_block[..., 3 + component, None, :] for component in range(3)]
    dist_sq = separation[0] * separation[0] + separation[1] * separation[1] + separation[2] * separation[2]
    support = jnp.maximum(1.0 - jnp.sqrt(dist_sq), 0.0)
    kernel_grad = -KERNEL * support * support * support
    closing = relative[0] * separation[0] + relative[1] * separation[1] + relative[2] * separation[2]
    approach = SMOOTH * closing / (dist_sq + 0.01 * SMOOTH * SMOOTH)
    dens_left = left_block[..., 6, :, None]
    dens_right = right_block[..., 6, None, :]
    visc_term = -ARTIFICIAL * SOUND_SPEED * jnp.minimum(approach, 0.0) * 2.0 / (dens_left + dens_right)
    scalar_term = (pressure_term(dens_left) + pressure_term(dens_right) + visc_term) * kernel_grad
    flux_term = closing * kernel_grad
    mass_left = left_block[..., 7, :, None]
    mass_right = right_block[..., 7, None, :]
    near_force = scalar_term * mass_right
    far_force = scalar_term * mass_left
    left_rates = jnp.stack([lax.optimization_barrier(jnp.sum(flux_term * mass_right, -1))] + [-lax.optimization_barrier(jnp.sum(near_force * sep, -1)) for sep in separation], -2)
    right_rates = jnp.stack([lax.optimization_barrier(jnp.sum(flux_term * mass_left, -2))] + [lax.optimization_barrier(jnp.sum(far_force * sep, -2)) for sep in separation], -2)
    return (left_rates, right_rates)

def evaluate(packed, pairs):
    baseline = jnp.zeros((8, 1, 1, 1, 1), jnp.float32).at[6].set(1.0)
    padded = jnp.pad(packed - baseline, ((0, 0), (1, 1), (1, 1), (1, 1), (0, 0))) + baseline
    own_rows = jnp.moveaxis(packed, 0, 3).reshape(GA, GC * GD, 8, BLOCK)
    summed = jnp.zeros((GA, GC * GD, 4, BLOCK), jnp.float32)
    for offset_id in range(27):
        step_a = offset_id // 9 - 1
        step_c = offset_id // 3 % 3 - 1
        step_d = offset_id % 3 - 1
        neighbour = padded[:, 1 + step_a:1 + step_a + GA, 1 + step_c:1 + step_c + GC, 1 + step_d:1 + step_d + GD]
        neighbour = jnp.moveaxis(neighbour, 0, 3).reshape(GA, GC * GD, 8, BLOCK)
        shift_vec = jnp.array([[step_a, step_c, step_d]], jnp.float32)

        def one_slab(slab_rows, shift_vec=shift_vec):
            return pair_terms(slab_rows[0], slab_rows[1], shift_vec)[0]
        gained = lax.map(one_slab, (own_rows, neighbour))
        if offset_id == 13:
            summed = summed + gained
        else:
            listed_id = offset_id if offset_id < 13 else offset_id - 1
            weight = pairs[listed_id].reshape(GA, GC * GD).astype(jnp.float32)[:, :, None, None]
            summed = summed + weight * gained
    summed = summed + jnp.array(GRAVITY, jnp.float32).reshape(1, 1, 4, 1)
    return jnp.moveaxis(summed.reshape(GA, GC, GD, 4, BLOCK), 3, 0)

def reference(offsets, velocity, density, mass, pairs):
    half_step = 0.5 * TIME_STEP
    packed = jnp.concatenate([offsets, velocity, density[None], mass[None]], 0)
    first_rates = evaluate(packed, pairs)
    moved_offsets = offsets + half_step * velocity
    velocity_half = velocity + half_step * first_rates[1:]
    density_half = density + half_step * first_rates[0]
    packed_half = jnp.concatenate([moved_offsets, velocity_half, density_half[None], mass[None]], 0)
    second_rates = evaluate(packed_half, pairs)
    velocity_corr = velocity + half_step * second_rates[1:]
    density_corr = density + half_step * second_rates[0]
    offsets_corr = offsets + half_step * velocity_corr
    advanced = jnp.concatenate([2.0 * offsets_corr - offsets, 2.0 * velocity_corr - velocity, (2.0 * density_corr - density)[None]], 0)
    return (second_rates, advanced)
```

```python
import math

import jax
import jax.numpy as jnp
import numpy as np
from jax import lax
from jax.experimental import pallas as pl
from jax.experimental.pallas import tpu as pltpu
from jax.sharding import PartitionSpec as P

SMOOTH = 0.5
SOUND_SPEED = 10.0
ARTIFICIAL = 0.5
TIME_STEP = 0.01
HALF = 0.5 * TIME_STEP
STIFFNESS = SOUND_SPEED * SOUND_SPEED / 7.0
KERNEL = 105.0 / (16.0 * math.pi * SMOOTH**5)
SOFT = 0.01 * SMOOTH * SMOOTH
VISC = -1.0 / (ARTIFICIAL * SOUND_SPEED * 2.0 * SMOOTH)
MESH = pl.DeviceIdType.MESH
F32 = jnp.float32
BF16 = jnp.bfloat16
W = 128
CHUNK = 32


def shift_table():
    table = np.zeros((9, 80, 2 * W), np.float32)
    for oa in (-1, 0, 1):
        for oc in (-1, 0, 1):
            entry = table[(oa + 1) * 3 + oc + 1]
            for start in (0, 8, 16):
                entry[start : start + 2, :W] = [[2 * oa], [2 * oc]]
                entry[start + 6, :W] = 1
                entry[start + 3 : start + 5, W:] = [[oa], [oc]]
                entry[start + 7, W:] = 1
            for start in (24, 32, 40):
                entry[start : start + 2, :W] = [[-2 * oa], [-2 * oc]]
                entry[start + 3 : start + 5, W:] = [[-oa], [-oc]]
            entry[48, :W] = oa * oa + oc * oc
    return table


def split3(value):
    top = value.astype(BF16).astype(F32)
    rest = value - top
    mid = rest.astype(BF16).astype(F32)
    return top, mid, rest - mid


def derive(raw, layer):
    row = lax.broadcasted_iota(jnp.int32, (8, W), 0)
    lift = (0.0, -1.0, 1.0)[layer]
    state = raw + jnp.where(row == 2, lift, 0.0) if lift else raw
    place = state[0:3]
    speed = state[3:6]
    square = place * place
    mixed = place * speed
    length = square[0:1] + square[1:2] + square[2:3]
    along = mixed[0:1] + mixed[1:2] + mixed[2:3]
    dens = state[6:7]
    mass = state[7:8]
    two = dens * dens
    four = two * two
    press = STIFFNESS * (four * two * dens - 1.0) / two
    plain = jnp.concatenate([place, VISC * dens, press, mass, jnp.zeros((2, W), F32)], 0)
    moments = jnp.concatenate([state[0:6], length, along], 0)
    return moments, plain


def right_tiles(parts):
    row = lax.broadcasted_iota(jnp.int32, (8, W), 0)
    near = []
    mixed = []
    for number, part in enumerate(parts):
        one = 1.0 if number == 0 else 0.0
        near.append(jnp.where(row < 3, -2.0 * part, jnp.where(row == 6, one, 0.0)))
        swapped = jnp.where(row < 3, pltpu.roll(part, 5, 0), pltpu.roll(part, 3, 0))
        mixed.append(jnp.where(row < 6, -swapped, jnp.where(row == 7, one, 0.0)))
    top = jnp.concatenate([jnp.concatenate([near[0], near[1]], 0), jnp.concatenate([mixed[0], mixed[1]], 0)], 1)
    low = jnp.concatenate([jnp.concatenate([near[2], near[0]], 0), jnp.concatenate([mixed[2], mixed[0]], 0)], 1)
    fixed = jnp.concatenate([top.astype(BF16), low.astype(BF16)], 0)
    moved = jnp.concatenate([parts[0], parts[1], parts[2], jnp.ones((8, W), F32)], 0).astype(BF16)
    return fixed, moved


def pair_chunk(dist_sq, closing, col, row, mass_row):
    safe = jnp.maximum(dist_sq, 1e-12)
    reach = jnp.maximum(1.0 - safe * lax.rsqrt(safe), 0.0)
    weight = (reach * reach * reach) * (col[5] * mass_row)
    visc = jnp.minimum(closing, 0.0) / ((safe + SOFT) * (col[3] + row[3]))
    force = weight * (visc + (col[4] + row[4]))
    return [force * (col[0] - row[0]), force * (col[1] - row[1]), force * (col[2] - row[2]), weight * closing]


def fold(values):
    total = values[0:8]
    for start in range(8, values.shape[0], 8):
        total = total + values[start : start + 8]
    return total


def step_kernel(
    counts, off, vel, den, mas, flags, table, rates, adv,
    raw, fixed, moved, plain, lefts, cols, acc_l, acc_r, net, own,
    in_a, in_cp, in_cm, in_d, send_sem, recv_sem,
):
    ai = lax.axis_index("along")
    ci = lax.axis_index("cross")
    di = lax.axis_index("depth")
    n_a, n_c = counts
    prev_a = {"along": lax.rem(ai + n_a - 1, n_a)}
    next_a = {"along": lax.rem(ai + 1, n_a)}
    prev_c = {"cross": lax.rem(ci + n_c - 1, n_c)}
    next_c = {"cross": lax.rem(ci + 1, n_c)}
    other = {"depth": 1 - di}
    sign = (1 - 2 * di).astype(F32)

    barrier = pltpu.get_barrier_semaphore()
    for device in (prev_a, next_a, prev_c, next_c, other):
        pl.semaphore_signal(barrier, inc=1, device_id=device, device_id_type=MESH)
    pl.semaphore_wait(barrier, 5)

    def depth_of(layer):
        return (1 - di) + layer * (2 * di - 1)

    row_id = lax.broadcasted_iota(jnp.int32, (8, W), 0)
    lane_id = lax.broadcasted_iota(jnp.int32, (W, W), 1)
    mirror = jnp.where((row_id == 2) | (row_id == 5), -1.0, 1.0)
    gravity = jnp.where(row_id == 3, 0.35, jnp.where(row_id == 5, -0.94 * sign, 0.0))
    gravity = jnp.where(row_id == 3, 0.35, gravity)
    zero8 = jnp.zeros((8, W), F32)

    def copy(kind, e, src, dst, device):
        return pltpu.make_async_remote_copy(
            src_ref=src, dst_ref=dst, send_sem=send_sem.at[e, kind], recv_sem=recv_sem.at[e, kind],
            device_id=device, device_id_type=MESH,
        )

    def copies(e):
        return (
            copy(0, e, raw.at[e, 0:4, 1:5, 0], raw.at[e, 0:4, 1:5, 2], other),
            copy(1, e, raw.at[e, 0:4, 1], raw.at[e, 0:4, 5], prev_c),
            copy(2, e, raw.at[e, 0, 4], raw.at[e, 0, 0], next_c),
            copy(3, e, raw.at[e, 0], raw.at[e, 4], prev_a),
            copy(4, e, net.at[e, 4], in_a.at[e], next_a),
            copy(5, e, net.at[e, 0:4, 5], in_cp.at[e], next_c),
            copy(6, e, net.at[e, 0, 0], in_cm.at[e], prev_c),
            copy(7, e, net.at[e, 0:4, 1:5, 2], in_d.at[e], other),
        )

    def prepare_right(e, a, c, layer):
        moments, flat = derive(raw[e, a, c, layer], layer)
        parts = split3(moments)
        solid, loose = right_tiles(parts)
        fixed[a, c, layer] = solid
        moved[a, c, layer] = loose
        plain[a, c, layer] = flat
        return parts, flat

    def prepare_own(e, a, c):
        for layer in (0, 1):
            parts, flat = prepare_right(e, a, c + 1, layer)
            d0, d1, d2 = parts
            one = jnp.ones((8, W), F32)
            stack = jnp.concatenate(
                [d0, d0, d1, d1, d0, d2, one, one, one, d0, d1, d2, one, zero8, zero8, flat], 0
            )
            turned = stack.T
            lefts[a * 4 + c, layer * W : layer * W + W] = turned.astype(BF16)
            cols[a * 4 + c, layer * W : layer * W + W] = turned

    def right_side(entry, a, c, layer):
        solid = fixed[a, c, layer]
        loose = moved[a, c, layer]
        bent = jnp.concatenate([loose, loose], 1) * table[entry, 0:32]
        return jnp.concatenate([solid[0:16], solid[0:16], solid[16:32], bent, table[entry, 32:80]], 0)

    def flag_of(base, a, c, layer, right_layer):
        step = (1, 0, 2)[right_layer] - (1, 0, 2)[layer]
        skipped = (1 + (1 - 2 * di) * step) // 2 if isinstance(base, int) else base // 13
        listed = base + 1 + (1 - 2 * di) * step - skipped
        return flags[listed * 32 + (a * 4 + c) * 2 + depth_of(layer)].astype(F32)

    def tiles(p, a, c, qa, qc, entry, base, shift, work, first=False, own_pairs=()):
        left_total = {}
        for right_layer, left_layers, both in work:
            lo, hi = min(left_layers), max(left_layers) + 1
            product = jnp.dot(
                lefts[p, lo * W : hi * W], right_side(entry, qa, qc, right_layer), preferred_element_type=F32
            )
            flat = plain[qa, qc, right_layer]
            placed = flat + shift
            rows = [placed[k : k + 1] for k in range(5)]
            right_total = None
            for layer in left_layers:
                mass_row = flat[5:6]
                if (layer, right_layer) not in own_pairs:
                    mass_row = mass_row * flag_of(base, a, c, layer, right_layer)
                for start in range(0, W, CHUNK):
                    spot = layer * W + start
                    here = product[spot - lo * W : spot - lo * W + CHUNK]
                    col = [cols[p, spot : spot + CHUNK, 120 + k : 121 + k] for k in range(6)]
                    terms = pair_chunk(here[:, :W], here[:, W:], col, rows, mass_row)
                    key = spot
                    if key in left_total:
                        left_total[key] = [x + y for x, y in zip(left_total[key], terms)]
                    else:
                        left_total[key] = terms
                    if layer in both:
                        folded = [fold(x) for x in terms]
                        right_total = folded if right_total is None else [x + y for x, y in zip(right_total, folded)]
            if right_total is not None:
                for k in range(4):
                    acc_r[qa, qc, right_layer, k] += right_total[k]
        for spot, terms in left_total.items():
            for k in range(4):
                if first:
                    acc_l[p, k, spot : spot + CHUNK] = terms[k]
                else:
                    acc_l[p, k, spot : spot + CHUNK] += terms[k]

    def reduced(a, c, layer):
        terms = [jnp.sum(acc_r[a, c, layer, k], 0, keepdims=True) for k in range(4)]
        return jnp.concatenate([jnp.zeros((3, W), F32)] + terms + [jnp.zeros((1, W), F32)], 0)

    def loop(count, body):
        def run(index, carry):
            body(index)
            return carry
        lax.fori_loop(0, count, run, 0)

    def fill(index):
        a, c = index // 4, index % 4
        for layer in (0, 1):
            at = pl.ds(depth_of(layer), 1)
            lines = [off[k, a, c, at, :] - 0.5 for k in range(3)] + [vel[k, a, c, at, :] for k in range(3)]
            lines += [den[a, c, at, :], mas[a, c, at, :]]
            lines[2] = lines[2] * sign
            lines[5] = lines[5] * sign
            raw[0, a, c + 1, layer] = jnp.concatenate(lines, 0)

    loop(16, fill)

    def evaluate(e):
        halo_d, halo_cm, halo_cp, halo_a, back_a, back_cp, back_cm, back_d = copies(e)
        halo_d.start()

        def first_part(index):
            prepare_own(e, index // 4, index % 4)

        loop(16, first_part)

        def clear(index):
            for c in range(6):
                for layer in range(3):
                    for k in range(4):
                        acc_r[index, c, layer, k] = zero8

        loop(5, clear)

        def self_part(index):
            a, c = index // 4, index % 4
            tiles(index, a, c, a, c + 1, 4, 12, 0.0, ((0, (0, 1), (1,)), (1, (1,), ())), True, ((0, 0), (1, 1)))

        loop(16, self_part)

        halo_d.wait_recv()

        def flip(index):
            a, c = index // 4, index % 4
            raw[e, a, c + 1, 2] = raw[e, a, c + 1, 2] * mirror

        loop(16, flip)
        halo_cm.start()
        halo_cp.start()

        def prepare_above(index):
            prepare_right(e, index // 4, index % 4 + 1, 2)

        loop(16, prepare_above)

        def above_part(index):
            a, c = index // 2, index % 2 + 2 * di
            tiles(a * 4 + c, a, c, a, c + 1, 4, 12, 0.0, ((2, (0,), (0,)),))

        loop(8, above_part)

        def pair_part(it):
            @pl.when(it == 12)
            def _():
                halo_cm.wait_recv()
                halo_cp.wait_recv()
                halo_a.start()

            @pl.when(it == 24)
            def _():
                halo_a.wait_recv()

                def side(index):
                    for layer in range(3):
                        prepare_right(e, index, 5, layer)

                def front(index):
                    for layer in range(3):
                        prepare_right(e, 4, index, layer)

                loop(4, side)
                loop(6, front)

            @pl.when(it == 46)
            def _():
                def give(index):
                    for layer in range(3):
                        net[e, 4, index, layer] = reduced(4, index, layer)

                loop(6, give)
                back_a.start()

            @pl.when(it == 55)
            def _():
                back_a.wait_recv()
                for layer in range(3):
                    net[e, 0, 0, layer] = reduced(0, 0, layer) + in_a[e, 0, layer]

                def give(index):
                    for layer in range(3):
                        net[e, index, 5, layer] = reduced(index, 5, layer)

                loop(4, give)
                for layer in range(3):
                    net[e, 0, 5, layer] += in_a[e, 5, layer]
                back_cp.start()
                back_cm.start()

            def pick(values, default):
                for limit, value in reversed(values):
                    default = jnp.where(it < limit, value, default)
                return default

            a = pick(
                ((12, it // 3), (24, (it - 12) // 4), (28, it - 24), (31, it - 28), (34, it - 30), (46, 3),
                 (55, (it - 46) // 3)), (it - 55) // 3)
            c = pick(
                ((12, it % 3), (24, it % 4), (34, 3), (46, (it - 34) % 4), (55, (it - 46) % 3)), 1 + (it - 55) % 3)
            oa = pick(((12, 0), (24, 1), (28, 0), (31, 1), (34, -1)), 1)
            oc = pick(((12, 1), (24, 0), (34, 1), (38, 0), (42, 1), (46, -1), (55, 1)), -1)
            base = (oa + 1) * 9 + (oc + 1) * 3
            entry = (oa + 1) * 3 + oc + 1
            shift = jnp.where(row_id == 0, oa.astype(F32), jnp.where(row_id == 1, oc.astype(F32), 0.0))
            tiles(a * 4 + c, a, c, a + oa, c + 1 + oc, entry, base, shift,
                  ((0, (0, 1), (0, 1)), (1, (0, 1), (0, 1)), (2, (0,), (0,))))

        loop(64, pair_part)

        back_cp.wait_recv()
        back_cm.wait_recv()

        def give_above(index):
            a, c = index // 4, index % 4
            net[e, a, c + 1, 2] = reduced(a, c + 1, 2)

        loop(16, give_above)
        for c in range(4):
            net[e, 0, c + 1, 2] += in_a[e, c + 1, 2]
        for a in range(4):
            net[e, a, 1, 2] += in_cp[e, a, 2]
        net[e, 0, 4, 2] += in_cm[e, 2]
        back_d.start()

        def collect(index):
            a, c = index // 4, index % 4
            for layer in (0, 1):
                sums = [acc_l[index, k, layer * W : layer * W + W] for k in range(4)]
                sums = [x + pltpu.roll(x, 64, 1) for x in sums]
                pairs = [jnp.where(lane_id < 64, sums[0], sums[1]), jnp.where(lane_id < 64, sums[2], sums[3])]
                pairs = [x + pltpu.roll(x, turn, 1) for x, turn in zip(pairs, (96, 32))]
                turned = jnp.where(lane_id % 64 < 32, pairs[0], pairs[1]).T
                lines = [jnp.sum(fold(turned[start : start + 32]), 0, keepdims=True) for start in (0, 64, 32, 96)]
                left = jnp.concatenate(
                    [jnp.zeros((3, W), F32), -lines[0], -lines[1], -lines[2], lines[3], jnp.zeros((1, W), F32)], 0)
                own[a, c, layer] = left + reduced(a, c + 1, layer)

        loop(16, collect)
        for c in range(4):
            for layer in (0, 1):
                own[0, c, layer] += in_a[e, c + 1, layer]
        for a in range(4):
            for layer in (0, 1):
                own[a, 0, layer] += in_cp[e, a, layer]
        for layer in (0, 1):
            own[0, 3, layer] += in_cm[e, layer]
        back_d.wait_recv()

        def finish(index):
            a, c = index // 4, index % 4
            for layer in (0, 1):
                state = raw[0, a, c + 1, layer]
                total = own[a, c, layer]
                if layer == 0:
                    total = total + in_d[e, a, c] * mirror
                rate = total * (-KERNEL / state[7:8]) + gravity
                speed = state + HALF * rate
                keep = (row_id >= 3) & (row_id < 7)

                @pl.when(e == 0)
                def _():
                    moved_place = state + HALF * pltpu.roll(state, 5, 0)
                    raw[1, a, c + 1, layer] = jnp.where(keep, speed, jnp.where(row_id < 3, moved_place, state))

                @pl.when(e == 1)
                def _():
                    at = pl.ds(depth_of(layer), 1)
                    start = jnp.where(row_id == 2, state * sign, state)
                    start = jnp.where(row_id < 3, start + 0.5, start)
                    start = jnp.where(row_id == 5, start * sign, start)
                    rate_g = jnp.where(row_id == 5, rate * sign, rate)
                    corr = start + HALF * rate_g
                    place = start + HALF * pltpu.roll(corr, 5, 0)
                    new = jnp.where(row_id < 3, 2.0 * place - start, 2.0 * corr - start)
                    for k in range(7):
                        adv[k, a, c, at, :] = new[k : k + 1]
                    rates[0, a, c, at, :] = rate_g[6:7]
                    for k in range(3):
                        rates[k + 1, a, c, at, :] = rate_g[3 + k : 4 + k]

        loop(16, finish)
        for item in (halo_d, halo_cm, halo_cp, halo_a, back_a, back_cp, back_cm, back_d):
            item.wait_send()

    loop(2, evaluate)


def shards(counts, offsets, velocity, density, mass, pairs):
    table = jnp.asarray(shift_table(), BF16)
    vmem = pl.BlockSpec(memory_space=pltpu.VMEM)
    smem = pl.BlockSpec(memory_space=pltpu.SMEM)

    def body(*refs):
        step_kernel(counts, *refs)

    return pl.pallas_call(
        body,
        out_shape=(
            jax.ShapeDtypeStruct((4, 4, 4, 2, W), F32),
            jax.ShapeDtypeStruct((7, 4, 4, 2, W), F32),
        ),
        in_specs=[vmem, vmem, vmem, vmem, smem, vmem],
        out_specs=(vmem, vmem),
        scratch_shapes=[
            pltpu.VMEM((2, 5, 6, 3, 8, W), F32),
            pltpu.VMEM((5, 6, 3, 32, 2 * W), BF16),
            pltpu.VMEM((5, 6, 3, 32, W), BF16),
            pltpu.VMEM((5, 6, 3, 8, W), F32),
            pltpu.VMEM((16, 2 * W, W), BF16),
            pltpu.VMEM((16, 2 * W, W), F32),
            pltpu.VMEM((16, 4, 2 * W, W), F32),
            pltpu.VMEM((5, 6, 3, 4, 8, W), F32),
            pltpu.VMEM((2, 5, 6, 3, 8, W), F32),
            pltpu.VMEM((4, 4, 2, 8, W), F32),
            pltpu.VMEM((2, 6, 3, 8, W), F32),
            pltpu.VMEM((2, 4, 3, 8, W), F32),
            pltpu.VMEM((2, 3, 8, W), F32),
            pltpu.VMEM((2, 4, 4, 8, W), F32),
            pltpu.SemaphoreType.DMA((2, 8)),
            pltpu.SemaphoreType.DMA((2, 8)),
        ],
        compiler_params=pltpu.CompilerParams(
            collective_id=0, has_side_effects=True, vmem_limit_bytes=40 * 1024 * 1024
        ),
        name="sph_step",
    )(offsets, velocity, density, mass, pairs.reshape(-1), table)


def solution(mesh):
    counts = (mesh.shape["along"], mesh.shape["cross"])

    def run(*args):
        return shards(counts, *args)

    spec = P(None, "along", "cross", "depth", None)
    plain = P("along", "cross", "depth", None)
    return jax.shard_map(
        run,
        mesh=mesh,
        in_specs=(spec, spec, plain, plain, P(None, "along", "cross", "depth")),
        out_specs=(spec, spec),
        check_vma=False,
    )
```

```python
import math

import jax
import jax.numpy as jnp
import numpy as np
from jax import lax
from jax.experimental import pallas as pl
from jax.experimental.pallas import tpu as pltpu
from jax.sharding import PartitionSpec as P

SMOOTH = 0.5
SOUND_SPEED = 10.0
ARTIFICIAL = 0.5
TIME_STEP = 0.01
HALF = 0.5 * TIME_STEP
STIFFNESS = SOUND_SPEED * SOUND_SPEED / 7.0
KERNEL = 105.0 / (16.0 * math.pi * SMOOTH**5)
SOFT = 0.01 * SMOOTH * SMOOTH
VISC = -1.0 / (ARTIFICIAL * SOUND_SPEED * 2.0 * SMOOTH)
MESH = pl.DeviceIdType.MESH
F32 = jnp.float32
BF16 = jnp.bfloat16
W = 128
CHUNK = 32
CENTRE = 4


def shift_rows(oa, oc):
    row = lax.broadcasted_iota(jnp.int32, (80, 2 * W), 0)
    near = lax.broadcasted_iota(jnp.int32, (80, 2 * W), 1) < W
    part = row % 8
    scale = jnp.where(near, 2.0, 1.0) * jnp.where(row < 24, 1.0, -1.0)
    first = jnp.where(near, 0, 3)
    one = jnp.where(near, 6, 7)
    value = jnp.where(part == first, oa * scale, jnp.where(part == first + 1, oc * scale, 0.0))
    value = jnp.where((part == one) & (row < 24), 1.0, value)
    last = jnp.where((row == 48) & near, oa * oa + oc * oc, 0.0)
    return jnp.where(row < 48, value, last).astype(BF16)


def split3(value):
    top = value.astype(BF16).astype(F32)
    rest = value - top
    mid = rest.astype(BF16).astype(F32)
    return top, mid, rest - mid


def derive(raw, layer):
    row = lax.broadcasted_iota(jnp.int32, (8, W), 0)
    lift = (0.0, -1.0, 1.0)[layer]
    state = raw + jnp.where(row == 2, lift, 0.0) if lift else raw
    place = state[0:3]
    speed = state[3:6]
    square = place * place
    mixed = place * speed
    length = square[0:1] + square[1:2] + square[2:3]
    along = mixed[0:1] + mixed[1:2] + mixed[2:3]
    dens = state[6:7]
    mass = state[7:8]
    two = dens * dens
    four = two * two
    press = STIFFNESS * (four * two * dens - 1.0) / two
    plain = jnp.concatenate([place, VISC * dens, press, mass, jnp.zeros((2, W), F32)], 0)
    moments = jnp.concatenate([state[0:6], length, along], 0)
    return moments, plain


def right_tiles(parts):
    row = lax.broadcasted_iota(jnp.int32, (8, W), 0)
    near = []
    mixed = []
    for number, part in enumerate(parts):
        one = 1.0 if number == 0 else 0.0
        near.append(jnp.where(row < 3, -2.0 * part, jnp.where(row == 6, one, 0.0)))
        swapped = jnp.where(row < 3, pltpu.roll(part, 5, 0), pltpu.roll(part, 3, 0))
        mixed.append(jnp.where(row < 6, -swapped, jnp.where(row == 7, one, 0.0)))
    top = jnp.concatenate([jnp.concatenate([near[0], near[1]], 0), jnp.concatenate([mixed[0], mixed[1]], 0)], 1)
    low = jnp.concatenate([jnp.concatenate([near[2], near[0]], 0), jnp.concatenate([mixed[2], mixed[0]], 0)], 1)
    fixed = jnp.concatenate([top.astype(BF16), low.astype(BF16)], 0)
    moved = jnp.concatenate([parts[0], parts[1], parts[2], jnp.ones((8, W), F32)], 0).astype(BF16)
    return fixed, moved


def pair_chunk(dist_sq, closing, col, row, mass_row):
    safe = jnp.maximum(dist_sq, 1e-12)
    reach = jnp.maximum(1.0 - safe * lax.rsqrt(safe), 0.0)
    weight = (reach * reach * reach) * (col[5] * mass_row)
    visc = jnp.minimum(closing, 0.0) / ((safe + SOFT) * (col[3] + row[3]))
    force = weight * (visc + (col[4] + row[4]))
    return [force * (col[0] - row[0]), force * (col[1] - row[1]), force * (col[2] - row[2]), weight * closing]


def fold(values):
    total = values[0:8]
    for start in range(8, values.shape[0], 8):
        total = total + values[start : start + 8]
    return total


def step_kernel(
    counts, off, vel, den, mas, flags, rates, adv,
    table, shifts, spread, picks, ready, raw, fixed, moved, plain, lefts, cols, acc_l, acc_r, net, own,
    in_a, in_cp, in_cm, in_d, send_sem, recv_sem,
):
    ai = lax.axis_index("along")
    ci = lax.axis_index("cross")
    di = lax.axis_index("depth")
    n_a, n_c = counts
    prev_a = {"along": lax.rem(ai + n_a - 1, n_a)}
    next_a = {"along": lax.rem(ai + 1, n_a)}
    prev_c = {"cross": lax.rem(ci + n_c - 1, n_c)}
    next_c = {"cross": lax.rem(ci + 1, n_c)}
    other = {"depth": 1 - di}
    sign = (1 - 2 * di).astype(F32)

    barrier = pltpu.get_barrier_semaphore()
    for device in (prev_a, next_a, prev_c, next_c, other):
        pl.semaphore_signal(barrier, inc=1, device_id=device, device_id_type=MESH)
    pl.semaphore_wait(barrier, 5)

    def depth_of(layer):
        return (1 - di) + layer * (2 * di - 1)

    row_id = lax.broadcasted_iota(jnp.int32, (8, W), 0)
    lane_id = lax.broadcasted_iota(jnp.int32, (W, W), 1)
    mirror = jnp.where((row_id == 2) | (row_id == 5), -1.0, 1.0)
    gravity = jnp.where(row_id == 3, 0.35, jnp.where(row_id == 5, -0.94 * sign, 0.0))
    gravity = jnp.where(row_id == 3, 0.35, gravity)
    zero8 = jnp.zeros((8, W), F32)

    def copy(kind, e, src, dst, device):
        return pltpu.make_async_remote_copy(
            src_ref=src, dst_ref=dst, send_sem=send_sem.at[e, kind], recv_sem=recv_sem.at[e, kind],
            device_id=device, device_id_type=MESH,
        )

    def copies(e):
        return (
            copy(0, e, raw.at[e, 0:4, 1:5, 0], raw.at[e, 0:4, 1:5, 2], other),
            copy(1, e, raw.at[e, 0:4, 1], raw.at[e, 0:4, 5], prev_c),
            copy(2, e, raw.at[e, 0, 4], raw.at[e, 0, 0], next_c),
            copy(3, e, raw.at[e, 0], raw.at[e, 4], prev_a),
            copy(4, e, net.at[e, 4], in_a.at[e], next_a),
            copy(5, e, net.at[e, 0:4, 5], in_cp.at[e], next_c),
            copy(6, e, net.at[e, 0, 0], in_cm.at[e], prev_c),
            copy(7, e, net.at[e, 0:4, 1:5, 2], in_d.at[e], other),
        )

    def prepare_right(e, a, c, layer):
        moments, flat = derive(raw[e, a, c, layer], layer)
        parts = split3(moments)
        solid, loose = right_tiles(parts)
        slot = (a * 6 + c) * 3 + layer
        fixed[slot] = solid
        moved[slot] = loose
        plain[slot] = flat
        return parts, flat

    def prepare_own(e, a, c):
        one = jnp.ones((8, W), F32)
        for layer in (0, 1):
            parts, flat = prepare_right(e, a, c + 1, layer)
            d0, d1, d2 = parts
            f0, f1, f2 = split3(flat)
            stack = jnp.concatenate([d0, d0, d1, d1, d0, d2, one, one, one, d0, d1, d2, one, f0, f1, f2], 0)
            lefts[a * 4 + c, layer * W : layer * W + W] = stack.T.astype(BF16)
        wide = jnp.dot(lefts[a * 4 + c], spread[...], preferred_element_type=F32)
        for k in range(6):
            cols[a * 4 + c, k] = wide[:, k * W : k * W + W]

    def right_side(entry, slot):
        solid = fixed[slot]
        loose = moved[slot]
        bent = jnp.concatenate([loose, loose], 1) * table[entry, 0:32]
        return jnp.concatenate([solid[0:16], solid[0:16], solid[16:32], bent, table[entry, 32:80]], 0)

    def flag_place(layer, right_layer):
        step = (1, 0, 2)[right_layer] - (1, 0, 2)[layer]
        return (1 - 2 * di) * step * 32 + depth_of(layer)

    places = {pair: flag_place(*pair) for pair in ((0, 0), (0, 1), (0, 2), (1, 0), (1, 1))}

    def tiles(p, q, entry, core, work, first=False, own_pairs=(), follow=None):
        left_total = {}
        for right_layer, left_layers, both in work:
            lo, hi = min(left_layers), max(left_layers) + 1
            product = None
            if follow is None:
                product = jnp.dot(
                    lefts[p, lo * W : hi * W], right_side(entry, q + right_layer), preferred_element_type=F32
                )
            flat = plain[q + right_layer]
            placed = flat if entry is CENTRE else flat + shifts[entry]
            rows = [placed[k : k + 1] for k in range(5)]
            right_total = None
            for layer in left_layers:
                mass_row = flat[5:6]
                if (layer, right_layer) not in own_pairs:
                    mass_row = mass_row * flags[core + places[layer, right_layer]].astype(F32)
                for start in range(0, W, CHUNK):
                    spot = layer * W + start
                    if product is None:
                        here = ready[right_layer * 2 * W + spot : right_layer * 2 * W + spot + CHUNK]
                    else:
                        here = product[spot - lo * W : spot - lo * W + CHUNK]
                    col = [cols[p, k, spot : spot + CHUNK] for k in range(6)]
                    terms = pair_chunk(here[:, :W], here[:, W:], col, rows, mass_row)
                    key = spot
                    if key in left_total:
                        left_total[key] = [x + y for x, y in zip(left_total[key], terms)]
                    else:
                        left_total[key] = terms
                    if layer in both:
                        folded = [fold(x) for x in terms]
                        right_total = folded if right_total is None else [x + y for x, y in zip(right_total, folded)]
            if right_total is not None:
                for k in range(4):
                    acc_r[q + right_layer, k] += right_total[k]
        if follow is not None:
            follow()
        for spot, terms in left_total.items():
            for k in range(4):
                if first:
                    acc_l[p, k, spot : spot + CHUNK] = terms[k]
                else:
                    acc_l[p, k, spot : spot + CHUNK] += terms[k]

    def reduced(a, c, layer):
        slot = (a * 6 + c) * 3 + layer
        terms = [jnp.sum(acc_r[slot, k], 0, keepdims=True) for k in range(4)]
        return jnp.concatenate([jnp.zeros((3, W), F32)] + terms + [jnp.zeros((1, W), F32)], 0)

    def loop(count, body):
        def run(index, carry):
            body(index)
            return carry
        lax.fori_loop(0, count, run, 0)

    def fill(index):
        a, c = index // 4, index % 4
        for layer in (0, 1):
            at = pl.ds(depth_of(layer), 1)
            lines = [off[k, a, c, at, :] - 0.5 for k in range(3)] + [vel[k, a, c, at, :] for k in range(3)]
            lines += [den[a, c, at, :], mas[a, c, at, :]]
            lines[2] = lines[2] * sign
            lines[5] = lines[5] * sign
            raw[0, a, c + 1, layer] = jnp.concatenate(lines, 0)

    def fill_table(index):
        oa, oc = (index // 3 - 1).astype(F32), (index % 3 - 1).astype(F32)
        table[index] = shift_rows(oa, oc)
        shifts[index] = jnp.where(row_id == 0, oa, jnp.where(row_id == 1, oc, 0.0))

    loop(9, fill_table)
    feature = lax.broadcasted_iota(jnp.int32, (W, W), 0)
    for k in range(6):
        spread[:, k * W : k * W + W] = jnp.where((feature >= 104) & (feature % 8 == k), 1.0, 0.0).astype(BF16)
    pick_row = lax.broadcasted_iota(jnp.int32, (16, 2 * W), 0)
    upper = lax.broadcasted_iota(jnp.int32, (16, 2 * W), 1) % W // 64
    picks[0] = jnp.where(pick_row == 3 + upper, -1.0, 0.0).astype(BF16)
    picks[1] = jnp.where(pick_row == 5 + upper, jnp.where(upper == 0, -1.0, 1.0), 0.0).astype(BF16)
    loop(16, fill)

    def evaluate(e):
        halo_d, halo_cm, halo_cp, halo_a, back_a, back_cp, back_cm, back_d = copies(e)
        halo_d.start()

        def first_part(index):
            for c in (0, 1):
                prepare_own(e, index // 2, index % 2 * 2 + c)

        loop(8, first_part)

        def clear(index):
            for number in range(18):
                for k in range(4):
                    acc_r[index * 18 + number, k] = zero8

        loop(5, clear)

        halo_d.wait_recv()

        def flip(index):
            a, c = index // 4, index % 4
            raw[e, a, c + 1, 2] = raw[e, a, c + 1, 2] * mirror

        loop(16, flip)
        halo_cm.start()
        halo_cp.start()

        def prepare_above(index):
            prepare_right(e, index // 4, index % 4 + 1, 2)

        loop(16, prepare_above)

        def column_part(index):
            a = index // 2

            def where_is(c):
                return a * 4 + c, (a * 6 + c + 1) * 3, (13 - di) * 32 - (1 - 2 * di) * 32 + (a * 4 + c) * 2

            for c in (index % 2, index % 2 + 2):
                p, q, core = where_is(c)
                tiles(p, q, CENTRE, core, ((0, (0, 1), (1,)), (1, (1,), ())), True, ((0, 0), (1, 1)))
            p, q, core = where_is(index % 2 + 2 * di)
            tiles(p, q, CENTRE, core, ((2, (0,), (0,)),))

        loop(8, column_part)

        def pick(values, default, at):
            for limit, value in reversed(values):
                default = jnp.where(at < limit, value, default)
            return default

        def locate(it):
            a = pick(
                ((12, it // 3), (24, (it - 12) // 4), (28, it - 24), (31, it - 28), (34, it - 30), (46, 3),
                 (55, (it - 46) // 3)), (it - 55) // 3, it)
            c = pick(
                ((12, it % 3), (24, it % 4), (34, 3), (46, (it - 34) % 4), (55, (it - 46) % 3)), 1 + (it - 55) % 3, it)
            oa = pick(((12, 0), (24, 1), (28, 0), (31, 1), (34, -1)), 1, it)
            oc = pick(((12, 1), (24, 0), (34, 1), (38, 0), (42, 1), (46, -1), (55, 1)), -1, it)
            base = (oa + 1) * 9 + (oc + 1) * 3
            core = (base + 1 - base // 13) * 32 + (a * 4 + c) * 2
            return a * 4 + c, ((a + oa) * 6 + c + 1 + oc) * 3, (oa + 1) * 3 + oc + 1, core

        def lead(place):
            p, q, entry, core = place
            for layer, rows in ((0, 2 * W), (1, 2 * W), (2, W)):
                ready[layer * 2 * W : layer * 2 * W + rows] = jnp.dot(
                    lefts[p, 0:rows], right_side(entry, q + layer), preferred_element_type=F32
                )

        def pair_part(it, carry):
            place, following = carry
            tiles(*place, ((0, (0, 1), (0, 1)), (1, (0, 1), (0, 1)), (2, (0,), (0,))), follow=lambda: lead(following))
            return following, locate(lax.rem(it + 2, 64))

        def phase_part(phase, carry):

            @pl.when(phase == 1)
            def _():
                halo_cm.wait_recv()
                halo_cp.wait_recv()
                halo_a.start()

            @pl.when(phase == 2)
            def _():
                halo_a.wait_recv()

                def side(index):
                    for layer in range(3):
                        prepare_right(e, index, 5, layer)

                def front(index):
                    for layer in range(3):
                        prepare_right(e, 4, index, layer)

                loop(4, side)
                loop(6, front)

            @pl.when(phase == 3)
            def _():
                def give(index):
                    for layer in range(3):
                        net[e, 4, index, layer] = reduced(4, index, layer)

                loop(6, give)
                back_a.start()

            @pl.when(phase == 4)
            def _():
                back_a.wait_recv()
                for layer in range(3):
                    net[e, 0, 0, layer] = reduced(0, 0, layer) + in_a[e, 0, layer]

                def give(index):
                    for layer in range(3):
                        net[e, index, 5, layer] = reduced(index, 5, layer)

                loop(4, give)
                for layer in range(3):
                    net[e, 0, 5, layer] += in_a[e, 5, layer]
                back_cp.start()
                back_cm.start()

            start, stop = (pick(((1, x), (2, y), (3, z), (4, w)), v, phase) for x, y, z, w, v in zip(
                (0, 11), (11, 23), (23, 46), (46, 55), (55, 64)))
            return lax.fori_loop(start, stop, pair_part, carry)

        begin = locate(jnp.int32(0))
        lead(begin)
        lax.fori_loop(0, 5, phase_part, (begin, locate(jnp.int32(1))))

        back_cp.wait_recv()
        back_cm.wait_recv()

        def give_above(index):
            a, c = index // 4, index % 4
            net[e, a, c + 1, 2] = reduced(a, c + 1, 2)

        loop(16, give_above)
        for c in range(4):
            net[e, 0, c + 1, 2] += in_a[e, c + 1, 2]
        for a in range(4):
            net[e, a, 1, 2] += in_cp[e, a, 2]
        net[e, 0, 4, 2] += in_cm[e, 2]
        back_d.start()

        def collect(number):
            for index in (number * 2, number * 2 + 1):
                a, c = index // 4, index % 4
                halves = [[], []]
                for layer in (0, 1):
                    sums = [acc_l[index, k, layer * W : layer * W + W] for k in range(4)]
                    low = lane_id < 64
                    for half, (x, y) in zip(halves, (sums[0:2], sums[2:4])):
                        both = jnp.where(low, x, y) + pltpu.roll(jnp.where(low, y, x), 64, 1)
                        top = both.astype(BF16)
                        half.append(jnp.concatenate([top, (both - top.astype(F32)).astype(BF16)], 1))
                left = None
                for number_of_half, half in enumerate(halves):
                    part = lax.dot_general(
                        picks[number_of_half], jnp.concatenate(half, 0), (((1,), (1,)), ((), ())),
                        preferred_element_type=F32,
                    )
                    left = part if left is None else left + part
                for layer in (0, 1):
                    own[a, c, layer] = left[0:8, layer * W : layer * W + W] + reduced(a, c + 1, layer)

        loop(8, collect)
        for c in range(4):
            for layer in (0, 1):
                own[0, c, layer] += in_a[e, c + 1, layer]
        for a in range(4):
            for layer in (0, 1):
                own[a, 0, layer] += in_cp[e, a, layer]
        for layer in (0, 1):
            own[0, 3, layer] += in_cm[e, layer]
        back_d.wait_recv()

        def finish(index):
            a, c = index // 4, index % 4
            for layer in (0, 1):
                state = raw[0, a, c + 1, layer]
                total = own[a, c, layer]
                if layer == 0:
                    total = total + in_d[e, a, c] * mirror
                rate = total * (-KERNEL / state[7:8]) + gravity
                speed = state + HALF * rate
                keep = (row_id >= 3) & (row_id < 7)

                @pl.when(e == 0)
                def _():
                    moved_place = state + HALF * pltpu.roll(state, 5, 0)
                    raw[1, a, c + 1, layer] = jnp.where(keep, speed, jnp.where(row_id < 3, moved_place, state))

                @pl.when(e == 1)
                def _():
                    at = pl.ds(depth_of(layer), 1)
                    start = jnp.where(row_id == 2, state * sign, state)
                    start = jnp.where(row_id < 3, start + 0.5, start)
                    start = jnp.where(row_id == 5, start * sign, start)
                    rate_g = jnp.where(row_id == 5, rate * sign, rate)
                    corr = start + HALF * rate_g
                    place = start + HALF * pltpu.roll(corr, 5, 0)
                    new = jnp.where(row_id < 3, 2.0 * place - start, 2.0 * corr - start)
                    for k in range(7):
                        adv[k, a, c, at, :] = new[k : k + 1]
                    rates[0, a, c, at, :] = rate_g[6:7]
                    for k in range(3):
                        rates[k + 1, a, c, at, :] = rate_g[3 + k : 4 + k]

        loop(16, finish)
        for item in (halo_d, halo_cm, halo_cp, halo_a, back_a, back_cp, back_cm, back_d):
            item.wait_send()

    loop(2, evaluate)


def shards(counts, offsets, velocity, density, mass, pairs):
    vmem = pl.BlockSpec(memory_space=pltpu.VMEM)
    smem = pl.BlockSpec(memory_space=pltpu.SMEM)

    def body(*refs):
        step_kernel(counts, *refs)

    return pl.pallas_call(
        body,
        out_shape=(
            jax.ShapeDtypeStruct((4, 4, 4, 2, W), F32),
            jax.ShapeDtypeStruct((7, 4, 4, 2, W), F32),
        ),
        in_specs=[vmem, vmem, vmem, vmem, smem],
        out_specs=(vmem, vmem),
        scratch_shapes=[
            pltpu.VMEM((9, 80, 2 * W), BF16),
            pltpu.VMEM((9, 8, W), F32),
            pltpu.VMEM((W, 6 * W), BF16),
            pltpu.VMEM((2, 16, 2 * W), BF16),
            pltpu.VMEM((5 * W, 2 * W), F32),
            pltpu.VMEM((2, 5, 6, 3, 8, W), F32),
            pltpu.VMEM((90, 32, 2 * W), BF16),
            pltpu.VMEM((90, 32, W), BF16),
            pltpu.VMEM((90, 8, W), F32),
            pltpu.VMEM((16, 2 * W, W), BF16),
            pltpu.VMEM((16, 6, 2 * W, W), F32),
            pltpu.VMEM((16, 4, 2 * W, W), F32),
            pltpu.VMEM((90, 4, 8, W), F32),
            pltpu.VMEM((2, 5, 6, 3, 8, W), F32),
            pltpu.VMEM((4, 4, 2, 8, W), F32),
            pltpu.VMEM((2, 6, 3, 8, W), F32),
            pltpu.VMEM((2, 4, 3, 8, W), F32),
            pltpu.VMEM((2, 3, 8, W), F32),
            pltpu.VMEM((2, 4, 4, 8, W), F32),
            pltpu.SemaphoreType.DMA((2, 8)),
            pltpu.SemaphoreType.DMA((2, 8)),
        ],
        compiler_params=pltpu.CompilerParams(
            collective_id=0, has_side_effects=True, vmem_limit_bytes=40 * 1024 * 1024
        ),
        name="sph_step",
    )(offsets, velocity, density, mass, pairs.reshape(-1))


def solution(mesh):
    counts = (mesh.shape["along"], mesh.shape["cross"])

    def run(*args):
        return shards(counts, *args)

    spec = P(None, "along", "cross", "depth", None)
    plain = P("along", "cross", "depth", None)
    return jax.shard_map(
        run,
        mesh=mesh,
        in_specs=(spec, spec, plain, plain, P(None, "along", "cross", "depth")),
        out_specs=(spec, spec),
        check_vma=False,
    )
```

```python
import math

import jax
import jax.numpy as jnp
import numpy as np
from jax import lax
from jax.experimental import pallas as pl
from jax.experimental.pallas import tpu as pltpu
from jax.sharding import PartitionSpec as P

SMOOTH = 0.5
SOUND_SPEED = 10.0
ARTIFICIAL = 0.5
TIME_STEP = 0.01
HALF = 0.5 * TIME_STEP
STIFFNESS = SOUND_SPEED * SOUND_SPEED / 7.0
KERNEL = 105.0 / (16.0 * math.pi * SMOOTH**5)
SOFT = 0.01 * SMOOTH * SMOOTH
VISC = -1.0 / (ARTIFICIAL * SOUND_SPEED * 2.0 * SMOOTH)
MESH = pl.DeviceIdType.MESH
F32 = jnp.float32
BF16 = jnp.bfloat16
W = 128
CHUNK = 8
CENTRE = 4


def shift_rows(oa, oc):
    row = lax.broadcasted_iota(jnp.int32, (80, 2 * W), 0)
    near = lax.broadcasted_iota(jnp.int32, (80, 2 * W), 1) < W
    part = row % 8
    scale = jnp.where(near, 2.0, 1.0) * jnp.where(row < 24, 1.0, -1.0)
    first = jnp.where(near, 0, 3)
    one = jnp.where(near, 6, 7)
    value = jnp.where(part == first, oa * scale, jnp.where(part == first + 1, oc * scale, 0.0))
    value = jnp.where((part == one) & (row < 24), 1.0, value)
    last = jnp.where((row == 48) & near, oa * oa + oc * oc, 0.0)
    return jnp.where(row < 48, value, last).astype(BF16)


def split3(value):
    top = value.astype(BF16).astype(F32)
    rest = value - top
    mid = rest.astype(BF16).astype(F32)
    return top, mid, rest - mid


def derive(raw, layer):
    row = lax.broadcasted_iota(jnp.int32, (8, W), 0)
    lift = (0.0, -1.0, 1.0)[layer]
    state = raw + jnp.where(row == 2, lift, 0.0) if lift else raw
    place = state[0:3]
    speed = state[3:6]
    square = place * place
    mixed = place * speed
    length = square[0:1] + square[1:2] + square[2:3]
    along = mixed[0:1] + mixed[1:2] + mixed[2:3]
    dens = state[6:7]
    mass = state[7:8]
    two = dens * dens
    four = two * two
    press = STIFFNESS * (four * two * dens - 1.0) / two
    plain = jnp.concatenate([place, VISC * dens, press, mass, jnp.zeros((2, W), F32)], 0)
    moments = jnp.concatenate([state[0:6], length, along], 0)
    return moments, plain


def right_tiles(parts):
    row = lax.broadcasted_iota(jnp.int32, (8, W), 0)
    near = []
    mixed = []
    for number, part in enumerate(parts):
        one = 1.0 if number == 0 else 0.0
        near.append(jnp.where(row < 3, -2.0 * part, jnp.where(row == 6, one, 0.0)))
        swapped = jnp.where(row < 3, pltpu.roll(part, 5, 0), pltpu.roll(part, 3, 0))
        mixed.append(jnp.where(row < 6, -swapped, jnp.where(row == 7, one, 0.0)))
    top = jnp.concatenate([jnp.concatenate([near[0], near[1]], 0), jnp.concatenate([mixed[0], mixed[1]], 0)], 1)
    low = jnp.concatenate([jnp.concatenate([near[2], near[0]], 0), jnp.concatenate([mixed[2], mixed[0]], 0)], 1)
    fixed = jnp.concatenate([top.astype(BF16), low.astype(BF16)], 0)
    moved = jnp.concatenate([parts[0], parts[1], parts[2], jnp.ones((8, W), F32)], 0).astype(BF16)
    return fixed, moved


def pair_chunk(dist_sq, closing, col, row, mass_row):
    safe = jnp.maximum(dist_sq, 1e-12)
    reach = jnp.maximum(1.0 - safe * lax.rsqrt(safe), 0.0)
    weight = (reach * reach * reach) * (col[5] * mass_row)
    visc = jnp.minimum(closing, 0.0) / ((safe + SOFT) * (col[3] + row[3]))
    force = weight * (visc + (col[4] + row[4]))
    return [force * (col[0] - row[0]), force * (col[1] - row[1]), force * (col[2] - row[2]), weight * closing]


def fold(values):
    total = values[0:8]
    for start in range(8, values.shape[0], 8):
        total = total + values[start : start + 8]
    return total


def step_kernel(
    counts, off, vel, den, mas, flags, rates, adv,
    table, shifts, spread, picks, ready, raw, fixed, moved, plain, lefts, cols, acc_l, acc_r, net, own,
    in_a, in_cp, in_cm, in_d, send_sem, recv_sem,
):
    ai = lax.axis_index("along")
    ci = lax.axis_index("cross")
    di = lax.axis_index("depth")
    n_a, n_c = counts
    prev_a = {"along": lax.rem(ai + n_a - 1, n_a)}
    next_a = {"along": lax.rem(ai + 1, n_a)}
    prev_c = {"cross": lax.rem(ci + n_c - 1, n_c)}
    next_c = {"cross": lax.rem(ci + 1, n_c)}
    other = {"depth": 1 - di}
    sign = (1 - 2 * di).astype(F32)

    barrier = pltpu.get_barrier_semaphore()
    for device in (prev_a, next_a, prev_c, next_c, other):
        pl.semaphore_signal(barrier, inc=1, device_id=device, device_id_type=MESH)
    pl.semaphore_wait(barrier, 5)

    def depth_of(layer):
        return (1 - di) + layer * (2 * di - 1)

    row_id = lax.broadcasted_iota(jnp.int32, (8, W), 0)
    lane_id = lax.broadcasted_iota(jnp.int32, (W, W), 1)
    mirror = jnp.where((row_id == 2) | (row_id == 5), -1.0, 1.0)
    gravity = jnp.where(row_id == 3, 0.35, jnp.where(row_id == 5, -0.94 * sign, 0.0))
    gravity = jnp.where(row_id == 3, 0.35, gravity)
    zero8 = jnp.zeros((8, W), F32)

    def copy(kind, e, src, dst, device):
        return pltpu.make_async_remote_copy(
            src_ref=src, dst_ref=dst, send_sem=send_sem.at[e, kind], recv_sem=recv_sem.at[e, kind],
            device_id=device, device_id_type=MESH,
        )

    def copies(e):
        return (
            copy(0, e, raw.at[e, 0:4, 1:5, 0], raw.at[e, 0:4, 1:5, 2], other),
            copy(1, e, raw.at[e, 0:4, 1], raw.at[e, 0:4, 5], prev_c),
            copy(2, e, raw.at[e, 0, 4], raw.at[e, 0, 0], next_c),
            copy(3, e, raw.at[e, 0], raw.at[e, 4], prev_a),
            copy(4, e, net.at[e, 4], in_a.at[e], next_a),
            copy(5, e, net.at[e, 0:4, 5], in_cp.at[e], next_c),
            copy(6, e, net.at[e, 0, 0], in_cm.at[e], prev_c),
            copy(7, e, net.at[e, 0:4, 1:5, 2], in_d.at[e], other),
        )

    def prepare_right(e, a, c, layer):
        moments, flat = derive(raw[e, a, c, layer], layer)
        parts = split3(moments)
        solid, loose = right_tiles(parts)
        slot = (a * 6 + c) * 3 + layer
        fixed[slot] = solid
        moved[slot] = loose
        plain[slot] = flat
        return parts, flat

    def prepare_own(e, a, c):
        one = jnp.ones((8, W), F32)
        for layer in (0, 1):
            parts, flat = prepare_right(e, a, c + 1, layer)
            d0, d1, d2 = parts
            f0, f1, f2 = split3(flat)
            stack = jnp.concatenate([d0, d0, d1, d1, d0, d2, one, one, one, d0, d1, d2, one, f0, f1, f2], 0)
            lefts[a * 4 + c, layer * W : layer * W + W] = stack.T.astype(BF16)
        wide = jnp.dot(lefts[a * 4 + c], spread[...], preferred_element_type=F32)
        for k in range(6):
            cols[a * 4 + c, k] = wide[:, k * W : k * W + W]

    def right_side(entry, slot):
        solid = fixed[slot]
        loose = moved[slot]
        bent = jnp.concatenate([loose, loose], 1) * table[entry, 0:32]
        return jnp.concatenate([solid[0:16], solid[0:16], solid[16:32], bent, table[entry, 32:80]], 0)

    def flag_place(layer, right_layer):
        step = (1, 0, 2)[right_layer] - (1, 0, 2)[layer]
        return (1 - 2 * di) * step * 32 + depth_of(layer)

    places = {pair: flag_place(*pair) for pair in ((0, 0), (0, 1), (0, 2), (1, 0), (1, 1))}

    def tiles(p, q, entry, core, work, first=False, own_pairs=(), buffer=None):
        products = {}
        if buffer is None:
            for right_layer, left_layers, both in work:
                lo, hi = min(left_layers), max(left_layers) + 1
                products[right_layer] = lo, jnp.dot(
                    lefts[p, lo * W : hi * W], right_side(entry, q + right_layer), preferred_element_type=F32
                )
        rows, masses = {}, {}
        for right_layer, left_layers, both in work:
            flat = plain[q + right_layer]
            placed = flat if entry is CENTRE else flat + shifts[entry]
            rows[right_layer] = [placed[k : k + 1] for k in range(5)]
            for layer in left_layers:
                mass_row = flat[5:6]
                if (layer, right_layer) not in own_pairs:
                    mass_row = mass_row * flags[core + places[layer, right_layer]].astype(F32)
                masses[layer, right_layer] = mass_row
        right_total = {}
        for layer in (0, 1):
            if not any(layer in left_layers for _, left_layers, _ in work):
                continue
            for start in range(0, W, CHUNK):
                spot = layer * W + start
                col = [cols[p, k, spot : spot + CHUNK] for k in range(6)]
                left_total = None
                for right_layer, left_layers, both in work:
                    if layer not in left_layers:
                        continue
                    if buffer is None:
                        lo, product = products[right_layer]
                        here = product[spot - lo * W : spot - lo * W + CHUNK]
                    else:
                        here = ready[buffer, right_layer * 2 * W + spot : right_layer * 2 * W + spot + CHUNK]
                    terms = pair_chunk(here[:, :W], here[:, W:], col, rows[right_layer], masses[layer, right_layer])
                    left_total = terms if left_total is None else [x + y for x, y in zip(left_total, terms)]
                    if layer in both:
                        folded = [fold(x) for x in terms]
                        old = right_total.get(right_layer)
                        right_total[right_layer] = folded if old is None else [x + y for x, y in zip(old, folded)]
                for k in range(4):
                    if first:
                        acc_l[p, k, spot : spot + CHUNK] = left_total[k]
                    else:
                        acc_l[p, k, spot : spot + CHUNK] += left_total[k]
        for right_layer, total in right_total.items():
            for k in range(4):
                acc_r[q + right_layer, k] += total[k]
    def reduced(a, c, layer):
        slot = (a * 6 + c) * 3 + layer
        terms = [jnp.sum(acc_r[slot, k], 0, keepdims=True) for k in range(4)]
        return jnp.concatenate([jnp.zeros((3, W), F32)] + terms + [jnp.zeros((1, W), F32)], 0)

    def loop(count, body):
        def run(index, carry):
            body(index)
            return carry
        lax.fori_loop(0, count, run, 0)

    def fill(index):
        a, c = index // 4, index % 4
        for layer in (0, 1):
            at = pl.ds(depth_of(layer), 1)
            lines = [off[k, a, c, at, :] - 0.5 for k in range(3)] + [vel[k, a, c, at, :] for k in range(3)]
            lines += [den[a, c, at, :], mas[a, c, at, :]]
            lines[2] = lines[2] * sign
            lines[5] = lines[5] * sign
            raw[0, a, c + 1, layer] = jnp.concatenate(lines, 0)

    def fill_table(index):
        oa, oc = (index // 3 - 1).astype(F32), (index % 3 - 1).astype(F32)
        table[index] = shift_rows(oa, oc)
        shifts[index] = jnp.where(row_id == 0, oa, jnp.where(row_id == 1, oc, 0.0))

    loop(9, fill_table)
    feature = lax.broadcasted_iota(jnp.int32, (W, W), 0)
    for k in range(6):
        spread[:, k * W : k * W + W] = jnp.where((feature >= 104) & (feature % 8 == k), 1.0, 0.0).astype(BF16)
    pick_row = lax.broadcasted_iota(jnp.int32, (16, 2 * W), 0)
    upper = lax.broadcasted_iota(jnp.int32, (16, 2 * W), 1) % W // 64
    picks[0] = jnp.where(pick_row == 3 + upper, -1.0, 0.0).astype(BF16)
    picks[1] = jnp.where(pick_row == 5 + upper, jnp.where(upper == 0, -1.0, 1.0), 0.0).astype(BF16)
    loop(16, fill)

    def evaluate(e):
        halo_d, halo_cm, halo_cp, halo_a, back_a, back_cp, back_cm, back_d = copies(e)
        halo_d.start()

        def first_part(index):
            for c in range(4):
                prepare_own(e, index, c)

        loop(4, first_part)

        def clear(index):
            for number in range(18):
                for k in range(4):
                    acc_r[index * 18 + number, k] = zero8

        loop(5, clear)

        halo_d.wait_recv()

        def flip(index):
            a, c = index // 4, index % 4
            raw[e, a, c + 1, 2] = raw[e, a, c + 1, 2] * mirror

        loop(16, flip)
        halo_cm.start()
        halo_cp.start()

        def prepare_above(index):
            prepare_right(e, index // 4, index % 4 + 1, 2)

        loop(16, prepare_above)

        def column_part(index):
            a = index

            def where_is(c):
                return a * 4 + c, (a * 6 + c + 1) * 3, (13 - di) * 32 - (1 - 2 * di) * 32 + (a * 4 + c) * 2

            for c in range(4):
                p, q, core = where_is(c)
                tiles(p, q, CENTRE, core, ((0, (0, 1), (1,)), (1, (1,), ())), True, ((0, 0), (1, 1)))
            for c in range(2):
                p, q, core = where_is(c + 2 * di)
                tiles(p, q, CENTRE, core, ((2, (0,), (0,)),))

        loop(4, column_part)

        def pick(values, default, at):
            for limit, value in reversed(values):
                default = jnp.where(at < limit, value, default)
            return default

        def locate(it):
            a = pick(
                ((12, it // 3), (24, (it - 12) // 4), (28, it - 24), (31, it - 28), (34, it - 30), (46, 3),
                 (55, (it - 46) // 3)), (it - 55) // 3, it)
            c = pick(
                ((12, it % 3), (24, it % 4), (34, 3), (46, (it - 34) % 4), (55, (it - 46) % 3)), 1 + (it - 55) % 3, it)
            oa = pick(((12, 0), (24, 1), (28, 0), (31, 1), (34, -1)), 1, it)
            oc = pick(((12, 1), (24, 0), (34, 1), (38, 0), (42, 1), (46, -1), (55, 1)), -1, it)
            base = (oa + 1) * 9 + (oc + 1) * 3
            core = (base + 1 - base // 13) * 32 + (a * 4 + c) * 2
            return a * 4 + c, ((a + oa) * 6 + c + 1 + oc) * 3, (oa + 1) * 3 + oc + 1, core

        def lead(place, buffer):
            p, q, entry, core = place
            for layer, rows in ((0, 2 * W), (1, 2 * W), (2, W)):
                ready[buffer, layer * 2 * W : layer * 2 * W + rows] = jnp.dot(
                    lefts[p, 0:rows], right_side(entry, q + layer), preferred_element_type=F32
                )

        def pair_part(number, carry):
            work = ((0, (0, 1), (0, 1)), (1, (0, 1), (0, 1)), (2, (0,), (0,)))
            for buffer in (0, 1):
                tiles(*carry[buffer], work, buffer=buffer)
            for buffer in (0, 1):
                lead(carry[2 + buffer], buffer)
            return carry[2], carry[3], locate(lax.rem(2 * number + 4, 64)), locate(lax.rem(2 * number + 5, 64))

        def phase_part(phase, carry):

            @pl.when(phase == 1)
            def _():
                halo_cm.wait_recv()
                halo_cp.wait_recv()
                halo_a.start()

            @pl.when(phase == 2)
            def _():
                halo_a.wait_recv()

                def side(index):
                    for layer in range(3):
                        prepare_right(e, index, 5, layer)

                def front(index):
                    for layer in range(3):
                        prepare_right(e, 4, index, layer)

                loop(4, side)
                loop(6, front)

            @pl.when(phase == 3)
            def _():
                def give(index):
                    for layer in range(3):
                        net[e, 4, index, layer] = reduced(4, index, layer)

                loop(6, give)
                back_a.start()

            @pl.when(phase == 4)
            def _():
                back_a.wait_recv()
                for layer in range(3):
                    net[e, 0, 0, layer] = reduced(0, 0, layer) + in_a[e, 0, layer]

                def give(index):
                    for layer in range(3):
                        net[e, index, 5, layer] = reduced(index, 5, layer)

                loop(4, give)
                for layer in range(3):
                    net[e, 0, 5, layer] += in_a[e, 5, layer]
                back_cp.start()
                back_cm.start()

            start, stop = (pick(((1, x), (2, y), (3, z), (4, w)), v, phase) for x, y, z, w, v in zip(
                (0, 5), (5, 11), (11, 23), (23, 27), (27, 32)))
            return lax.fori_loop(start, stop, pair_part, carry)

        begin = tuple(locate(jnp.int32(number)) for number in range(4))
        lead(begin[0], 0)
        lead(begin[1], 1)
        lax.fori_loop(0, 5, phase_part, begin)

        back_cp.wait_recv()
        back_cm.wait_recv()

        def give_above(index):
            a, c = index // 4, index % 4
            net[e, a, c + 1, 2] = reduced(a, c + 1, 2)

        loop(16, give_above)
        for c in range(4):
            net[e, 0, c + 1, 2] += in_a[e, c + 1, 2]
        for a in range(4):
            net[e, a, 1, 2] += in_cp[e, a, 2]
        net[e, 0, 4, 2] += in_cm[e, 2]
        back_d.start()

        def collect(number):
            for a, c in ((number, c) for c in range(4)):
                index = a * 4 + c
                halves = [[], []]
                for layer in (0, 1):
                    sums = [acc_l[index, k, layer * W : layer * W + W] for k in range(4)]
                    low = lane_id < 64
                    for half, (x, y) in zip(halves, (sums[0:2], sums[2:4])):
                        both = jnp.where(low, x, y) + pltpu.roll(jnp.where(low, y, x), 64, 1)
                        top = both.astype(BF16)
                        half.append(jnp.concatenate([top, (both - top.astype(F32)).astype(BF16)], 1))
                left = None
                for number_of_half, half in enumerate(halves):
                    part = lax.dot_general(
                        picks[number_of_half], jnp.concatenate(half, 0), (((1,), (1,)), ((), ())),
                        preferred_element_type=F32,
                    )
                    left = part if left is None else left + part
                for layer in (0, 1):
                    own[a, c, layer] = left[0:8, layer * W : layer * W + W] + reduced(a, c + 1, layer)

        loop(4, collect)
        for c in range(4):
            for layer in (0, 1):
                own[0, c, layer] += in_a[e, c + 1, layer]
        for a in range(4):
            for layer in (0, 1):
                own[a, 0, layer] += in_cp[e, a, layer]
        for layer in (0, 1):
            own[0, 3, layer] += in_cm[e, layer]
        back_d.wait_recv()

        def finish(index):
            a, c = index // 4, index % 4
            for layer in (0, 1):
                state = raw[0, a, c + 1, layer]
                total = own[a, c, layer]
                if layer == 0:
                    total = total + in_d[e, a, c] * mirror
                rate = total * (-KERNEL / state[7:8]) + gravity
                speed = state + HALF * rate
                keep = (row_id >= 3) & (row_id < 7)

                @pl.when(e == 0)
                def _():
                    moved_place = state + HALF * pltpu.roll(state, 5, 0)
                    raw[1, a, c + 1, layer] = jnp.where(keep, speed, jnp.where(row_id < 3, moved_place, state))

                @pl.when(e == 1)
                def _():
                    at = pl.ds(depth_of(layer), 1)
                    start = jnp.where(row_id == 2, state * sign, state)
                    start = jnp.where(row_id < 3, start + 0.5, start)
                    start = jnp.where(row_id == 5, start * sign, start)
                    rate_g = jnp.where(row_id == 5, rate * sign, rate)
                    corr = start + HALF * rate_g
                    place = start + HALF * pltpu.roll(corr, 5, 0)
                    new = jnp.where(row_id < 3, 2.0 * place - start, 2.0 * corr - start)
                    for k in range(7):
                        adv[k, a, c, at, :] = new[k : k + 1]
                    rates[0, a, c, at, :] = rate_g[6:7]
                    for k in range(3):
                        rates[k + 1, a, c, at, :] = rate_g[3 + k : 4 + k]

        loop(16, finish)
        for item in (halo_d, halo_cm, halo_cp, halo_a, back_a, back_cp, back_cm, back_d):
            item.wait_send()

    loop(2, evaluate)


def shards(counts, offsets, velocity, density, mass, pairs):
    vmem = pl.BlockSpec(memory_space=pltpu.VMEM)
    smem = pl.BlockSpec(memory_space=pltpu.SMEM)

    def body(*refs):
        step_kernel(counts, *refs)

    return pl.pallas_call(
        body,
        out_shape=(
            jax.ShapeDtypeStruct((4, 4, 4, 2, W), F32),
            jax.ShapeDtypeStruct((7, 4, 4, 2, W), F32),
        ),
        in_specs=[vmem, vmem, vmem, vmem, smem],
        out_specs=(vmem, vmem),
        scratch_shapes=[
            pltpu.VMEM((9, 80, 2 * W), BF16),
            pltpu.VMEM((9, 8, W), F32),
            pltpu.VMEM((W, 6 * W), BF16),
            pltpu.VMEM((2, 16, 2 * W), BF16),
            pltpu.VMEM((2, 5 * W, 2 * W), F32),
            pltpu.VMEM((2, 5, 6, 3, 8, W), F32),
            pltpu.VMEM((90, 32, 2 * W), BF16),
            pltpu.VMEM((90, 32, W), BF16),
            pltpu.VMEM((90, 8, W), F32),
            pltpu.VMEM((16, 2 * W, W), BF16),
            pltpu.VMEM((16, 6, 2 * W, W), F32),
            pltpu.VMEM((16, 4, 2 * W, W), F32),
            pltpu.VMEM((90, 4, 8, W), F32),
            pltpu.VMEM((2, 5, 6, 3, 8, W), F32),
            pltpu.VMEM((4, 4, 2, 8, W), F32),
            pltpu.VMEM((2, 6, 3, 8, W), F32),
            pltpu.VMEM((2, 4, 3, 8, W), F32),
            pltpu.VMEM((2, 3, 8, W), F32),
            pltpu.VMEM((2, 4, 4, 8, W), F32),
            pltpu.SemaphoreType.DMA((2, 8)),
            pltpu.SemaphoreType.DMA((2, 8)),
        ],
        compiler_params=pltpu.CompilerParams(
            collective_id=0, has_side_effects=True, vmem_limit_bytes=40 * 1024 * 1024
        ),
        name="sph_step",
    )(offsets, velocity, density, mass, pairs.reshape(-1))


def solution(mesh):
    counts = (mesh.shape["along"], mesh.shape["cross"])

    def run(*args):
        return shards(counts, *args)

    spec = P(None, "along", "cross", "depth", None)
    plain = P("along", "cross", "depth", None)
    return jax.shard_map(
        run,
        mesh=mesh,
        in_specs=(spec, spec, plain, plain, P(None, "along", "cross", "depth")),
        out_specs=(spec, spec),
        check_vma=False,
    )
```

```python
import math

import jax
import jax.numpy as jnp
import numpy as np
from jax import lax
from jax.experimental import pallas as pl
from jax.experimental.pallas import tpu as pltpu
from jax.sharding import PartitionSpec as P

SMOOTH = 0.5
SOUND_SPEED = 10.0
ARTIFICIAL = 0.5
TIME_STEP = 0.01
HALF = 0.5 * TIME_STEP
STIFFNESS = SOUND_SPEED * SOUND_SPEED / 7.0
KERNEL = 105.0 / (16.0 * math.pi * SMOOTH**5)
SOFT = 0.01 * SMOOTH * SMOOTH
VISC = -1.0 / (ARTIFICIAL * SOUND_SPEED * 2.0 * SMOOTH)
MESH = pl.DeviceIdType.MESH
F32 = jnp.float32
BF16 = jnp.bfloat16
W = 128
CHUNK = 8
CENTRE = 4


def shift_rows(oa, oc):
    row = lax.broadcasted_iota(jnp.int32, (80, 2 * W), 0)
    near = lax.broadcasted_iota(jnp.int32, (80, 2 * W), 1) < W
    part = row % 8
    scale = jnp.where(near, 2.0, 1.0) * jnp.where(row < 24, 1.0, -1.0)
    first = jnp.where(near, 0, 3)
    one = jnp.where(near, 6, 7)
    value = jnp.where(part == first, oa * scale, jnp.where(part == first + 1, oc * scale, 0.0))
    value = jnp.where((part == one) & (row < 24), 1.0, value)
    last = jnp.where((row == 48) & near, oa * oa + oc * oc, 0.0)
    return jnp.where(row < 48, value, last).astype(BF16)


def split3(value):
    top = value.astype(BF16).astype(F32)
    rest = value - top
    mid = rest.astype(BF16).astype(F32)
    return top, mid, rest - mid


def derive(raw, layer):
    row = lax.broadcasted_iota(jnp.int32, (8, W), 0)
    lift = (0.0, -1.0, 1.0)[layer]
    state = raw + jnp.where(row == 2, lift, 0.0) if lift else raw
    place = state[0:3]
    speed = state[3:6]
    square = place * place
    mixed = place * speed
    length = square[0:1] + square[1:2] + square[2:3]
    along = mixed[0:1] + mixed[1:2] + mixed[2:3]
    dens = state[6:7]
    mass = state[7:8]
    two = dens * dens
    four = two * two
    press = STIFFNESS * (four * two * dens - 1.0) / two
    plain = jnp.concatenate([place, VISC * dens, press, mass, jnp.zeros((2, W), F32)], 0)
    moments = jnp.concatenate([state[0:6], length, along], 0)
    return moments, plain


def right_tiles(parts):
    row = lax.broadcasted_iota(jnp.int32, (8, W), 0)
    near = []
    mixed = []
    for number, part in enumerate(parts):
        one = 1.0 if number == 0 else 0.0
        near.append(jnp.where(row < 3, -2.0 * part, jnp.where(row == 6, one, 0.0)))
        swapped = jnp.where(row < 3, pltpu.roll(part, 5, 0), pltpu.roll(part, 3, 0))
        mixed.append(jnp.where(row < 6, -swapped, jnp.where(row == 7, one, 0.0)))
    top = jnp.concatenate([jnp.concatenate([near[0], near[1]], 0), jnp.concatenate([mixed[0], mixed[1]], 0)], 1)
    low = jnp.concatenate([jnp.concatenate([near[2], near[0]], 0), jnp.concatenate([mixed[2], mixed[0]], 0)], 1)
    fixed = jnp.concatenate([top.astype(BF16), low.astype(BF16)], 0)
    moved = jnp.concatenate([parts[0], parts[1], parts[2], jnp.ones((8, W), F32)], 0).astype(BF16)
    return fixed, moved


def pair_chunk(dist_sq, closing, col, row, mass_row):
    safe = jnp.maximum(dist_sq, 1e-12)
    reach = jnp.maximum(1.0 - safe * lax.rsqrt(safe), 0.0)
    weight = (reach * reach * reach) * (col[5] * mass_row)
    visc = jnp.minimum(closing, 0.0) / ((safe + SOFT) * (col[3] + row[3]))
    force = weight * (visc + (col[4] + row[4]))
    return [force * (col[0] - row[0]), force * (col[1] - row[1]), force * (col[2] - row[2]), weight * closing]


def fold(values):
    total = values[0:8]
    for start in range(8, values.shape[0], 8):
        total = total + values[start : start + 8]
    return total


def step_kernel(
    counts, off, vel, den, mas, flags, rates, adv,
    table, shifts, spread, picks, ready, raw, fixed, moved, plain, lefts, cols, acc_l, acc_r, net, own,
    in_a, in_cp, in_cm, in_d, send_sem, recv_sem,
):
    ai = lax.axis_index("along")
    ci = lax.axis_index("cross")
    di = lax.axis_index("depth")
    n_a, n_c = counts
    prev_a = {"along": lax.rem(ai + n_a - 1, n_a)}
    next_a = {"along": lax.rem(ai + 1, n_a)}
    prev_c = {"cross": lax.rem(ci + n_c - 1, n_c)}
    next_c = {"cross": lax.rem(ci + 1, n_c)}
    other = {"depth": 1 - di}
    sign = (1 - 2 * di).astype(F32)

    barrier = pltpu.get_barrier_semaphore()
    for device in (prev_a, next_a, prev_c, next_c, other):
        pl.semaphore_signal(barrier, inc=1, device_id=device, device_id_type=MESH)

    def depth_of(layer):
        return (1 - di) + layer * (2 * di - 1)

    row_id = lax.broadcasted_iota(jnp.int32, (8, W), 0)
    lane_id = lax.broadcasted_iota(jnp.int32, (W, W), 1)
    mirror = jnp.where((row_id == 2) | (row_id == 5), -1.0, 1.0)
    gravity = jnp.where(row_id == 3, 0.35, jnp.where(row_id == 5, -0.94 * sign, 0.0))
    gravity = jnp.where(row_id == 3, 0.35, gravity)
    zero8 = jnp.zeros((8, W), F32)

    def copy(kind, e, src, dst, device):
        return pltpu.make_async_remote_copy(
            src_ref=src, dst_ref=dst, send_sem=send_sem.at[e, kind], recv_sem=recv_sem.at[e, kind],
            device_id=device, device_id_type=MESH,
        )

    def copies(e):
        return (
            copy(0, e, raw.at[e, 0:4, 1:5, 0], raw.at[e, 0:4, 1:5, 2], other),
            copy(1, e, raw.at[e, 0:4, 1], raw.at[e, 0:4, 5], prev_c),
            copy(2, e, raw.at[e, 0, 4], raw.at[e, 0, 0], next_c),
            copy(3, e, raw.at[e, 0], raw.at[e, 4], prev_a),
            copy(4, e, net.at[e, 4], in_a.at[e], next_a),
            copy(5, e, net.at[e, 0:4, 5], in_cp.at[e], next_c),
            copy(6, e, net.at[e, 0, 0], in_cm.at[e], prev_c),
            copy(7, e, net.at[e, 0:4, 1:5, 2], in_d.at[e], other),
        )

    def prepare_right(e, a, c, layer):
        moments, flat = derive(raw[e, a, c, layer], layer)
        parts = split3(moments)
        solid, loose = right_tiles(parts)
        slot = (a * 6 + c) * 3 + layer
        fixed[slot] = solid
        moved[slot] = loose
        plain[slot] = flat
        return parts, flat

    def prepare_own(e, a, c):
        one = jnp.ones((8, W), F32)
        for layer in (0, 1):
            parts, flat = prepare_right(e, a, c + 1, layer)
            d0, d1, d2 = parts
            f0, f1, f2 = split3(flat)
            stack = jnp.concatenate([d0, d0, d1, d1, d0, d2, one, one, one, d0, d1, d2, one, f0, f1, f2], 0)
            lefts[a * 4 + c, layer * W : layer * W + W] = stack.T.astype(BF16)

    def right_side(entry, slot):
        solid = fixed[slot]
        loose = moved[slot]
        bent = jnp.concatenate([loose, loose], 1) * table[entry, 0:32]
        return jnp.concatenate([solid[0:16], solid[0:16], solid[16:32], bent, table[entry, 32:80]], 0)

    def flag_place(layer, right_layer):
        step = (1, 0, 2)[right_layer] - (1, 0, 2)[layer]
        return (1 - 2 * di) * step * 32 + depth_of(layer)

    places = {pair: flag_place(*pair) for pair in ((0, 0), (0, 1), (0, 2), (1, 0), (1, 1))}

    def tiles(p, q, entry, core, work, first=False, own_pairs=(), buffer=None):
        products = {}
        if buffer is None:
            for right_layer, left_layers, both in work:
                lo, hi = min(left_layers), max(left_layers) + 1
                products[right_layer] = lo, jnp.dot(
                    lefts[p, lo * W : hi * W], right_side(entry, q + right_layer), preferred_element_type=F32
                )
        rows, masses = {}, {}
        for right_layer, left_layers, both in work:
            flat = plain[q + right_layer]
            placed = flat if entry is CENTRE else flat + shifts[entry]
            rows[right_layer] = [placed[k : k + 1] for k in range(5)]
            for layer in left_layers:
                mass_row = flat[5:6]
                if (layer, right_layer) not in own_pairs:
                    mass_row = mass_row * flags[core + places[layer, right_layer]].astype(F32)
                masses[layer, right_layer] = mass_row
        right_total = {}
        for layer in (0, 1):
            if not any(layer in left_layers for _, left_layers, _ in work):
                continue
            for start in range(0, W, CHUNK):
                spot = layer * W + start
                col = [cols[p, k, spot : spot + CHUNK] for k in range(6)]
                left_total = None
                for right_layer, left_layers, both in work:
                    if layer not in left_layers:
                        continue
                    if buffer is None:
                        lo, product = products[right_layer]
                        here = product[spot - lo * W : spot - lo * W + CHUNK]
                    else:
                        here = ready[buffer, right_layer * 2 * W + spot : right_layer * 2 * W + spot + CHUNK]
                    terms = pair_chunk(here[:, :W], here[:, W:], col, rows[right_layer], masses[layer, right_layer])
                    left_total = terms if left_total is None else [x + y for x, y in zip(left_total, terms)]
                    if layer in both:
                        folded = [fold(x) for x in terms]
                        old = right_total.get(right_layer)
                        right_total[right_layer] = folded if old is None else [x + y for x, y in zip(old, folded)]
                for k in range(4):
                    if first:
                        acc_l[p, k, spot : spot + CHUNK] = left_total[k]
                    else:
                        acc_l[p, k, spot : spot + CHUNK] += left_total[k]
        for right_layer, total in right_total.items():
            for k in range(4):
                acc_r[q + right_layer, k] += total[k]
    def reduced(a, c, layer):
        slot = (a * 6 + c) * 3 + layer
        terms = [jnp.sum(acc_r[slot, k], 0, keepdims=True) for k in range(4)]
        return jnp.concatenate([jnp.zeros((3, W), F32)] + terms + [jnp.zeros((1, W), F32)], 0)

    def loop(count, body):
        def run(index, carry):
            body(index)
            return carry
        lax.fori_loop(0, count, run, 0)

    def fill(a):
        for c, layer in ((c, layer) for c in range(4) for layer in (0, 1)):
            at = pl.ds(depth_of(layer), 1)
            lines = [off[k, a, c, at, :] - 0.5 for k in range(3)] + [vel[k, a, c, at, :] for k in range(3)]
            lines += [den[a, c, at, :], mas[a, c, at, :]]
            lines[2] = lines[2] * sign
            lines[5] = lines[5] * sign
            raw[0, a, c + 1, layer] = jnp.concatenate(lines, 0)

    def fill_table(index):
        oa, oc = (index // 3 - 1).astype(F32), (index % 3 - 1).astype(F32)
        table[index] = shift_rows(oa, oc)
        shifts[index] = jnp.where(row_id == 0, oa, jnp.where(row_id == 1, oc, 0.0))

    loop(9, fill_table)
    feature = lax.broadcasted_iota(jnp.int32, (W, W), 0)
    for k in range(6):
        spread[:, k * W : k * W + W] = jnp.where((feature >= 104) & (feature % 8 == k), 1.0, 0.0).astype(BF16)
    pick_row = lax.broadcasted_iota(jnp.int32, (16, 2 * W), 0)
    upper = lax.broadcasted_iota(jnp.int32, (16, 2 * W), 1) % W // 64
    picks[0] = jnp.where(pick_row == 3 + upper, -1.0, 0.0).astype(BF16)
    picks[1] = jnp.where(pick_row == 5 + upper, jnp.where(upper == 0, -1.0, 1.0), 0.0).astype(BF16)
    loop(4, fill)
    pl.semaphore_wait(barrier, 5)

    def evaluate(e):
        halo_d, halo_cm, halo_cp, halo_a, back_a, back_cp, back_cm, back_d = copies(e)
        halo_d.start()

        def first_part(index):
            for c in range(4):
                prepare_own(e, index, c)
            for c in (0, 2):
                both = lefts[pl.ds(index * 4 + c, 2)].reshape(4 * W, W)
                wide = jnp.dot(both, spread[...], preferred_element_type=F32)
                for k in range(6):
                    for half in (0, 1):
                        cols[index * 4 + c + half, k] = wide[half * 2 * W : half * 2 * W + 2 * W, k * W : k * W + W]

        loop(4, first_part)

        def clear(index):
            for number in range(18):
                for k in range(4):
                    acc_r[index * 18 + number, k] = zero8

        loop(5, clear)

        halo_d.wait_recv()

        def flip(a):
            for c in range(4):
                raw[e, a, c + 1, 2] = raw[e, a, c + 1, 2] * mirror

        loop(4, flip)
        halo_cm.start()
        halo_cp.start()

        def prepare_above(a):
            for c in range(4):
                prepare_right(e, a, c + 1, 2)

        loop(4, prepare_above)

        def column_part(index):
            a = index

            def where_is(c):
                return a * 4 + c, (a * 6 + c + 1) * 3, (13 - di) * 32 - (1 - 2 * di) * 32 + (a * 4 + c) * 2

            for c in range(4):
                p, q, core = where_is(c)
                tiles(p, q, CENTRE, core, ((0, (0, 1), (1,)), (1, (1,), ())), True, ((0, 0), (1, 1)))
            for c in range(2):
                p, q, core = where_is(c + 2 * di)
                tiles(p, q, CENTRE, core, ((2, (0,), (0,)),))

        loop(4, column_part)

        def pick(values, default, at):
            for limit, value in reversed(values):
                default = jnp.where(at < limit, value, default)
            return default

        def locate(it):
            a = pick(
                ((12, it // 3), (24, (it - 12) // 4), (28, it - 24), (31, it - 28), (34, it - 30), (46, 3),
                 (55, (it - 46) // 3)), (it - 55) // 3, it)
            c = pick(
                ((12, it % 3), (24, it % 4), (34, 3), (46, (it - 34) % 4), (55, (it - 46) % 3)), 1 + (it - 55) % 3, it)
            oa = pick(((12, 0), (24, 1), (28, 0), (31, 1), (34, -1)), 1, it)
            oc = pick(((12, 1), (24, 0), (34, 1), (38, 0), (42, 1), (46, -1), (55, 1)), -1, it)
            base = (oa + 1) * 9 + (oc + 1) * 3
            core = (base + 1 - base // 13) * 32 + (a * 4 + c) * 2
            return a * 4 + c, ((a + oa) * 6 + c + 1 + oc) * 3, (oa + 1) * 3 + oc + 1, core

        def lead(place, buffer):
            p, q, entry, core = place
            for layer, rows in ((0, 2 * W), (1, 2 * W), (2, W)):
                ready[buffer, layer * 2 * W : layer * 2 * W + rows] = jnp.dot(
                    lefts[p, 0:rows], right_side(entry, q + layer), preferred_element_type=F32
                )

        def pair_part(number, carry):
            work = ((0, (0, 1), (0, 1)), (1, (0, 1), (0, 1)), (2, (0,), (0,)))
            for buffer in (0, 1):
                tiles(*carry[buffer], work, buffer=buffer)
            for buffer in (0, 1):
                lead(carry[2 + buffer], buffer)
            return carry[2], carry[3], locate(lax.rem(2 * number + 4, 64)), locate(lax.rem(2 * number + 5, 64))

        def phase_part(phase, carry):

            @pl.when(phase == 1)
            def _():
                halo_cm.wait_recv()
                halo_cp.wait_recv()
                halo_a.start()

            @pl.when(phase == 2)
            def _():
                halo_a.wait_recv()

                def side(index):
                    for layer in range(3):
                        prepare_right(e, index, 5, layer)

                def front(index):
                    for layer in range(3):
                        prepare_right(e, 4, index, layer)

                loop(4, side)
                loop(6, front)

            @pl.when(phase == 3)
            def _():
                def give(index):
                    for layer in range(3):
                        net[e, 4, index, layer] = reduced(4, index, layer)

                loop(6, give)
                back_a.start()

            @pl.when(phase == 4)
            def _():
                back_a.wait_recv()
                for layer in range(3):
                    net[e, 0, 0, layer] = reduced(0, 0, layer) + in_a[e, 0, layer]

                def give(index):
                    for layer in range(3):
                        net[e, index, 5, layer] = reduced(index, 5, layer)

                loop(4, give)
                for layer in range(3):
                    net[e, 0, 5, layer] += in_a[e, 5, layer]
                back_cp.start()
                back_cm.start()

            start, stop = (pick(((1, x), (2, y), (3, z), (4, w)), v, phase) for x, y, z, w, v in zip(
                (0, 5), (5, 11), (11, 23), (23, 27), (27, 32)))
            return lax.fori_loop(start, stop, pair_part, carry)

        begin = tuple(locate(jnp.int32(number)) for number in range(4))
        lead(begin[0], 0)
        lead(begin[1], 1)
        lax.fori_loop(0, 5, phase_part, begin)

        back_cp.wait_recv()
        back_cm.wait_recv()

        def give_above(a):
            for c in range(4):
                net[e, a, c + 1, 2] = reduced(a, c + 1, 2)

        loop(4, give_above)
        for c in range(4):
            net[e, 0, c + 1, 2] += in_a[e, c + 1, 2]
        for a in range(4):
            net[e, a, 1, 2] += in_cp[e, a, 2]
        net[e, 0, 4, 2] += in_cm[e, 2]
        back_d.start()

        def collect(number):
            for a, c in ((number, c) for c in range(4)):
                index = a * 4 + c
                halves = [[], []]
                for layer in (0, 1):
                    sums = [acc_l[index, k, layer * W : layer * W + W] for k in range(4)]
                    low = lane_id < 64
                    for half, (x, y) in zip(halves, (sums[0:2], sums[2:4])):
                        both = jnp.where(low, x, y) + pltpu.roll(jnp.where(low, y, x), 64, 1)
                        top = both.astype(BF16)
                        half.append(jnp.concatenate([top, (both - top.astype(F32)).astype(BF16)], 1))
                left = None
                for number_of_half, half in enumerate(halves):
                    part = lax.dot_general(
                        picks[number_of_half], jnp.concatenate(half, 0), (((1,), (1,)), ((), ())),
                        preferred_element_type=F32,
                    )
                    left = part if left is None else left + part
                for layer in (0, 1):
                    own[a, c, layer] = left[0:8, layer * W : layer * W + W] + reduced(a, c + 1, layer)

        loop(4, collect)
        for c in range(4):
            for layer in (0, 1):
                own[0, c, layer] += in_a[e, c + 1, layer]
        for a in range(4):
            for layer in (0, 1):
                own[a, 0, layer] += in_cp[e, a, layer]
        for layer in (0, 1):
            own[0, 3, layer] += in_cm[e, layer]
        back_d.wait_recv()

        def settled(a, c, layer):
            state = raw[0, a, c + 1, layer]
            total = own[a, c, layer]
            if layer == 0:
                total = total + in_d[e, a, c] * mirror
            return state, total * (-KERNEL / state[7:8]) + gravity

        @pl.when(e == 0)
        def _():
            def half_way(a):
                keep = (row_id >= 3) & (row_id < 7)
                for c, layer in ((c, layer) for c in range(4) for layer in (0, 1)):
                    state, rate = settled(a, c, layer)
                    place = state + HALF * pltpu.roll(state, 5, 0)
                    raw[1, a, c + 1, layer] = jnp.where(
                        keep, state + HALF * rate, jnp.where(row_id < 3, place, state))

            loop(4, half_way)

        @pl.when(e == 1)
        def _():
            def finish(a):
                for c, layer in ((c, layer) for c in range(4) for layer in (0, 1)):
                    state, rate = settled(a, c, layer)
                    at = pl.ds(depth_of(layer), 1)
                    turn = jnp.where((row_id == 2) | (row_id == 5), sign, 1.0)
                    start = state * turn
                    start = jnp.where(row_id < 3, start + 0.5, start)
                    rate_g = rate * turn
                    corr = start + HALF * rate_g
                    place = start + HALF * pltpu.roll(corr, 5, 0)
                    new = jnp.where(row_id < 3, 2.0 * place - start, 2.0 * corr - start)
                    for k in range(7):
                        adv[k, a, c, at, :] = new[k : k + 1]
                    rates[0, a, c, at, :] = rate_g[6:7]
                    for k in range(3):
                        rates[k + 1, a, c, at, :] = rate_g[3 + k : 4 + k]

            loop(4, finish)

        for item in (halo_d, halo_cm, halo_cp, halo_a, back_a, back_cp, back_cm, back_d):
            item.wait_send()

    loop(2, evaluate)


def shards(counts, offsets, velocity, density, mass, pairs):
    vmem = pl.BlockSpec(memory_space=pltpu.VMEM)
    smem = pl.BlockSpec(memory_space=pltpu.SMEM)

    def body(*refs):
        step_kernel(counts, *refs)

    return pl.pallas_call(
        body,
        out_shape=(
            jax.ShapeDtypeStruct((4, 4, 4, 2, W), F32),
            jax.ShapeDtypeStruct((7, 4, 4, 2, W), F32),
        ),
        in_specs=[vmem, vmem, vmem, vmem, smem],
        out_specs=(vmem, vmem),
        scratch_shapes=[
            pltpu.VMEM((9, 80, 2 * W), BF16),
            pltpu.VMEM((9, 8, W), F32),
            pltpu.VMEM((W, 6 * W), BF16),
            pltpu.VMEM((2, 16, 2 * W), BF16),
            pltpu.VMEM((2, 5 * W, 2 * W), F32),
            pltpu.VMEM((2, 5, 6, 3, 8, W), F32),
            pltpu.VMEM((90, 32, 2 * W), BF16),
            pltpu.VMEM((90, 32, W), BF16),
            pltpu.VMEM((90, 8, W), F32),
            pltpu.VMEM((16, 2 * W, W), BF16),
            pltpu.VMEM((16, 6, 2 * W, W), F32),
            pltpu.VMEM((16, 4, 2 * W, W), F32),
            pltpu.VMEM((90, 4, 8, W), F32),
            pltpu.VMEM((2, 5, 6, 3, 8, W), F32),
            pltpu.VMEM((4, 4, 2, 8, W), F32),
            pltpu.VMEM((2, 6, 3, 8, W), F32),
            pltpu.VMEM((2, 4, 3, 8, W), F32),
            pltpu.VMEM((2, 3, 8, W), F32),
            pltpu.VMEM((2, 4, 4, 8, W), F32),
            pltpu.SemaphoreType.DMA((2, 8)),
            pltpu.SemaphoreType.DMA((2, 8)),
        ],
        compiler_params=pltpu.CompilerParams(
            collective_id=0, has_side_effects=True, vmem_limit_bytes=40 * 1024 * 1024
        ),
        name="sph_step",
    )(offsets, velocity, density, mass, pairs.reshape(-1))


def solution(mesh):
    counts = (mesh.shape["along"], mesh.shape["cross"])

    def run(*args):
        return shards(counts, *args)

    spec = P(None, "along", "cross", "depth", None)
    plain = P("along", "cross", "depth", None)
    return jax.shard_map(
        run,
        mesh=mesh,
        in_specs=(spec, spec, plain, plain, P(None, "along", "cross", "depth")),
        out_specs=(spec, spec),
        check_vma=False,
    )
```

```python
import math

import jax
import jax.numpy as jnp
import numpy as np
from jax import lax
from jax.experimental import pallas as pl
from jax.experimental.pallas import tpu as pltpu
from jax.sharding import PartitionSpec as P

SMOOTH = 0.5
SOUND_SPEED = 10.0
ARTIFICIAL = 0.5
TIME_STEP = 0.01
HALF = 0.5 * TIME_STEP
STIFFNESS = SOUND_SPEED * SOUND_SPEED / 7.0
KERNEL = 105.0 / (16.0 * math.pi * SMOOTH**5)
SOFT = 0.01 * SMOOTH * SMOOTH
VISC = -1.0 / (ARTIFICIAL * SOUND_SPEED * 2.0 * SMOOTH)
MESH = pl.DeviceIdType.MESH
F32 = jnp.float32
BF16 = jnp.bfloat16
W = 128
CHUNK = 8
CENTRE = 4


def shift_rows(oa, oc):
    row = lax.broadcasted_iota(jnp.int32, (80, 2 * W), 0)
    near = lax.broadcasted_iota(jnp.int32, (80, 2 * W), 1) < W
    part = row % 8
    scale = jnp.where(near, 2.0, 1.0) * jnp.where(row < 24, 1.0, -1.0)
    first = jnp.where(near, 0, 3)
    one = jnp.where(near, 6, 7)
    value = jnp.where(part == first, oa * scale, jnp.where(part == first + 1, oc * scale, 0.0))
    value = jnp.where((part == one) & (row < 24), 1.0, value)
    last = jnp.where((row == 48) & near, oa * oa + oc * oc, 0.0)
    return jnp.where(row < 48, value, last).astype(BF16)


def split3(value):
    top = value.astype(BF16).astype(F32)
    rest = value - top
    mid = rest.astype(BF16).astype(F32)
    return top, mid, rest - mid


def derive(raw, layer):
    row = lax.broadcasted_iota(jnp.int32, (8, W), 0)
    lift = (0.0, -1.0, 1.0)[layer]
    state = raw + jnp.where(row == 2, lift, 0.0) if lift else raw
    place = state[0:3]
    speed = state[3:6]
    square = place * place
    mixed = place * speed
    length = square[0:1] + square[1:2] + square[2:3]
    along = mixed[0:1] + mixed[1:2] + mixed[2:3]
    dens = state[6:7]
    mass = state[7:8]
    two = dens * dens
    four = two * two
    press = STIFFNESS * (four * two * dens - 1.0) / two
    plain = jnp.concatenate([place, VISC * dens, press, mass, jnp.zeros((2, W), F32)], 0)
    moments = jnp.concatenate([state[0:6], length, along], 0)
    return moments, plain


def right_tiles(parts):
    row = lax.broadcasted_iota(jnp.int32, (8, W), 0)
    near = []
    mixed = []
    for number, part in enumerate(parts):
        one = 1.0 if number == 0 else 0.0
        near.append(jnp.where(row < 3, -2.0 * part, jnp.where(row == 6, one, 0.0)))
        swapped = jnp.where(row < 3, pltpu.roll(part, 5, 0), pltpu.roll(part, 3, 0))
        mixed.append(jnp.where(row < 6, -swapped, jnp.where(row == 7, one, 0.0)))
    top = jnp.concatenate([jnp.concatenate([near[0], near[1]], 0), jnp.concatenate([mixed[0], mixed[1]], 0)], 1)
    low = jnp.concatenate([jnp.concatenate([near[2], near[0]], 0), jnp.concatenate([mixed[2], mixed[0]], 0)], 1)
    fixed = jnp.concatenate([top.astype(BF16), low.astype(BF16)], 0)
    moved = jnp.concatenate([parts[0], parts[1], parts[2], jnp.ones((8, W), F32)], 0).astype(BF16)
    return fixed, moved


def pair_chunk(dist_sq, closing, col, row, mass_row):
    safe = jnp.maximum(dist_sq, 1e-12)
    reach = jnp.maximum(1.0 - safe * lax.rsqrt(safe), 0.0)
    weight = (reach * reach * reach) * (col[5] * mass_row)
    visc = jnp.minimum(closing, 0.0) / ((safe + SOFT) * (col[3] + row[3]))
    force = weight * (visc + (col[4] + row[4]))
    return [force * (col[0] - row[0]), force * (col[1] - row[1]), force * (col[2] - row[2]), weight * closing]


def fold(values):
    total = values[0:8]
    for start in range(8, values.shape[0], 8):
        total = total + values[start : start + 8]
    return total


def step_kernel(
    counts, off, vel, den, mas, flags, rates, adv,
    table, shifts, spread, picks, ready, raw, fixed, moved, plain, lefts, cols, acc_l, acc_r, net, own,
    in_a, in_cp, in_cm, in_d, send_sem, recv_sem,
):
    ai = lax.axis_index("along")
    ci = lax.axis_index("cross")
    di = lax.axis_index("depth")
    n_a, n_c = counts
    prev_a = {"along": lax.rem(ai + n_a - 1, n_a)}
    next_a = {"along": lax.rem(ai + 1, n_a)}
    prev_c = {"cross": lax.rem(ci + n_c - 1, n_c)}
    next_c = {"cross": lax.rem(ci + 1, n_c)}
    other = {"depth": 1 - di}
    sign = (1 - 2 * di).astype(F32)

    barrier = pltpu.get_barrier_semaphore()
    for device in (prev_a, next_a, prev_c, next_c, other):
        pl.semaphore_signal(barrier, inc=1, device_id=device, device_id_type=MESH)

    def depth_of(layer):
        return (1 - di) + layer * (2 * di - 1)

    row_id = lax.broadcasted_iota(jnp.int32, (8, W), 0)
    lane_id = lax.broadcasted_iota(jnp.int32, (W, W), 1)
    mirror = jnp.where((row_id == 2) | (row_id == 5), -1.0, 1.0)
    gravity = jnp.where(row_id == 3, 0.35, jnp.where(row_id == 5, -0.94 * sign, 0.0))
    gravity = jnp.where(row_id == 3, 0.35, gravity)
    zero8 = jnp.zeros((8, W), F32)

    def copy(kind, e, src, dst, device):
        return pltpu.make_async_remote_copy(
            src_ref=src, dst_ref=dst, send_sem=send_sem.at[e, kind], recv_sem=recv_sem.at[e, kind],
            device_id=device, device_id_type=MESH,
        )

    def copies(e):
        return (
            copy(0, e, raw.at[e, 0:4, 1:5, 0], raw.at[e, 0:4, 1:5, 2], other),
            copy(1, e, raw.at[e, 0:4, 1], raw.at[e, 0:4, 5], prev_c),
            copy(2, e, raw.at[e, 0, 4], raw.at[e, 0, 0], next_c),
            copy(3, e, raw.at[e, 0], raw.at[e, 4], prev_a),
            copy(4, e, net.at[e, 4], in_a.at[e], next_a),
            copy(5, e, net.at[e, 0:4, 5], in_cp.at[e], next_c),
            copy(6, e, net.at[e, 0, 0], in_cm.at[e], prev_c),
            copy(7, e, net.at[e, 0:4, 1:5, 2], in_d.at[e], other),
        )

    def prepare_right(e, a, c, layer):
        moments, flat = derive(raw[e, a, c, layer], layer)
        parts = split3(moments)
        solid, loose = right_tiles(parts)
        slot = (a * 6 + c) * 3 + layer
        fixed[slot] = solid
        moved[slot] = loose
        plain[slot] = flat
        return parts, flat

    def prepare_own(e, a, c):
        one = jnp.ones((8, W), F32)
        for layer in (0, 1):
            parts, flat = prepare_right(e, a, c + 1, layer)
            d0, d1, d2 = parts
            f0, f1, f2 = split3(flat)
            tail = jnp.concatenate([one[0:1], flat[4:6], jnp.zeros((5, W), F32)], 0)
            stack = jnp.concatenate([d0, d0, d1, d1, d0, d2, one, one, one, d0, d1, d2, tail, f0, f1, f2], 0)
            turned = stack.T
            lefts[a * 4 + c, layer * W : layer * W + W] = turned.astype(BF16)
            for k in (4, 5):
                cols[a * 4 + c, k, layer * W : layer * W + W] = jnp.broadcast_to(turned[:, 93 + k : 94 + k], (W, W))

    def right_side(entry, slot):
        solid = fixed[slot]
        loose = moved[slot]
        bent = jnp.concatenate([loose, loose], 1) * table[entry, 0:32]
        return jnp.concatenate([solid[0:16], solid[0:16], solid[16:32], bent, table[entry, 32:80]], 0)

    def flag_place(layer, right_layer):
        step = (1, 0, 2)[right_layer] - (1, 0, 2)[layer]
        return (1 - 2 * di) * step * 32 + depth_of(layer)

    places = {pair: flag_place(*pair) for pair in ((0, 0), (0, 1), (0, 2), (1, 0), (1, 1))}

    def tiles(p, q, entry, core, work, first=False, own_pairs=(), buffer=None):
        products = {}
        if buffer is None:
            for right_layer, left_layers, both in work:
                lo, hi = min(left_layers), max(left_layers) + 1
                products[right_layer] = lo, jnp.dot(
                    lefts[p, lo * W : hi * W], right_side(entry, q + right_layer), preferred_element_type=F32
                )
        rows, masses = {}, {}
        for right_layer, left_layers, both in work:
            flat = plain[q + right_layer]
            placed = flat if entry is CENTRE else flat + shifts[entry]
            rows[right_layer] = [placed[k : k + 1] for k in range(5)]
            for layer in left_layers:
                mass_row = flat[5:6]
                if (layer, right_layer) not in own_pairs:
                    mass_row = mass_row * flags[core + places[layer, right_layer]].astype(F32)
                masses[layer, right_layer] = mass_row
        right_total = {}
        for layer in (0, 1):
            if not any(layer in left_layers for _, left_layers, _ in work):
                continue
            for start in range(0, W, CHUNK):
                spot = layer * W + start
                col = [cols[p, k, spot : spot + CHUNK] for k in range(6)]
                left_total = None
                for right_layer, left_layers, both in work:
                    if layer not in left_layers:
                        continue
                    if buffer is None:
                        lo, product = products[right_layer]
                        here = product[spot - lo * W : spot - lo * W + CHUNK]
                    else:
                        here = ready[buffer, right_layer * 2 * W + spot : right_layer * 2 * W + spot + CHUNK]
                    terms = pair_chunk(here[:, :W], here[:, W:], col, rows[right_layer], masses[layer, right_layer])
                    left_total = terms if left_total is None else [x + y for x, y in zip(left_total, terms)]
                    if layer in both:
                        folded = [fold(x) for x in terms]
                        old = right_total.get(right_layer)
                        right_total[right_layer] = folded if old is None else [x + y for x, y in zip(old, folded)]
                for k in range(4):
                    if first:
                        acc_l[p, k, spot : spot + CHUNK] = left_total[k]
                    else:
                        acc_l[p, k, spot : spot + CHUNK] += left_total[k]
        for right_layer, total in right_total.items():
            for k in range(4):
                acc_r[q + right_layer, k] += total[k]
    def reduced(a, c, layer):
        slot = (a * 6 + c) * 3 + layer
        terms = [jnp.sum(acc_r[slot, k], 0, keepdims=True) for k in range(4)]
        return jnp.concatenate([jnp.zeros((3, W), F32)] + terms + [jnp.zeros((1, W), F32)], 0)

    def loop(count, body):
        def run(index, carry):
            body(index)
            return carry
        lax.fori_loop(0, count, run, 0)

    def fill(a):
        for c, layer in ((c, layer) for c in range(4) for layer in (0, 1)):
            at = pl.ds(depth_of(layer), 1)
            lines = [off[k, a, c, at, :] - 0.5 for k in range(3)] + [vel[k, a, c, at, :] for k in range(3)]
            lines += [den[a, c, at, :], mas[a, c, at, :]]
            lines[2] = lines[2] * sign
            lines[5] = lines[5] * sign
            raw[0, a, c + 1, layer] = jnp.concatenate(lines, 0)

    def fill_table(index):
        oa, oc = (index // 3 - 1).astype(F32), (index % 3 - 1).astype(F32)
        table[index] = shift_rows(oa, oc)
        shifts[index] = jnp.where(row_id == 0, oa, jnp.where(row_id == 1, oc, 0.0))

    loop(9, fill_table)
    feature = lax.broadcasted_iota(jnp.int32, (W, W), 0)
    for k in range(4):
        spread[:, k * W : k * W + W] = jnp.where((feature >= 104) & (feature % 8 == k), 1.0, 0.0).astype(BF16)
    pick_row = lax.broadcasted_iota(jnp.int32, (16, 2 * W), 0)
    upper = lax.broadcasted_iota(jnp.int32, (16, 2 * W), 1) % W // 64
    picks[0] = jnp.where(pick_row == 3 + upper, -1.0, 0.0).astype(BF16)
    picks[1] = jnp.where(pick_row == 5 + upper, jnp.where(upper == 0, -1.0, 1.0), 0.0).astype(BF16)
    loop(4, fill)
    pl.semaphore_wait(barrier, 5)

    def evaluate(e):
        halo_d, halo_cm, halo_cp, halo_a, back_a, back_cp, back_cm, back_d = copies(e)
        halo_d.start()

        def first_part(index):
            for c in range(4):
                prepare_own(e, index, c)
            for c in (0, 2):
                both = lefts[pl.ds(index * 4 + c, 2)].reshape(4 * W, W)
                wide = jnp.dot(both, spread[...], preferred_element_type=F32)
                for k in range(4):
                    for half in (0, 1):
                        cols[index * 4 + c + half, k] = wide[half * 2 * W : half * 2 * W + 2 * W, k * W : k * W + W]

        loop(4, first_part)

        def clear(index):
            for number in range(18):
                for k in range(4):
                    acc_r[index * 18 + number, k] = zero8

        loop(5, clear)

        halo_d.wait_recv()

        def flip(a):
            for c in range(4):
                raw[e, a, c + 1, 2] = raw[e, a, c + 1, 2] * mirror

        loop(4, flip)
        halo_cm.start()
        halo_cp.start()

        def prepare_above(a):
            for c in range(4):
                prepare_right(e, a, c + 1, 2)

        loop(4, prepare_above)

        def column_part(index):
            a = index

            def where_is(c):
                return a * 4 + c, (a * 6 + c + 1) * 3, (13 - di) * 32 - (1 - 2 * di) * 32 + (a * 4 + c) * 2

            for c in range(4):
                p, q, core = where_is(c)
                tiles(p, q, CENTRE, core, ((0, (0, 1), (1,)), (1, (1,), ())), True, ((0, 0), (1, 1)))
            for c in range(2):
                p, q, core = where_is(c + 2 * di)
                tiles(p, q, CENTRE, core, ((2, (0,), (0,)),))

        loop(4, column_part)

        def pick(values, default, at):
            for limit, value in reversed(values):
                default = jnp.where(at < limit, value, default)
            return default

        def locate(it):
            a = pick(
                ((12, it // 3), (24, (it - 12) // 4), (28, it - 24), (31, it - 28), (34, it - 30), (46, 3),
                 (55, (it - 46) // 3)), (it - 55) // 3, it)
            c = pick(
                ((12, it % 3), (24, it % 4), (34, 3), (46, (it - 34) % 4), (55, (it - 46) % 3)), 1 + (it - 55) % 3, it)
            oa = pick(((12, 0), (24, 1), (28, 0), (31, 1), (34, -1)), 1, it)
            oc = pick(((12, 1), (24, 0), (34, 1), (38, 0), (42, 1), (46, -1), (55, 1)), -1, it)
            base = (oa + 1) * 9 + (oc + 1) * 3
            core = (base + 1 - base // 13) * 32 + (a * 4 + c) * 2
            return a * 4 + c, ((a + oa) * 6 + c + 1 + oc) * 3, (oa + 1) * 3 + oc + 1, core

        def lead(place, buffer):
            p, q, entry, core = place
            for layer, rows in ((0, 2 * W), (1, 2 * W), (2, W)):
                ready[buffer, layer * 2 * W : layer * 2 * W + rows] = jnp.dot(
                    lefts[p, 0:rows], right_side(entry, q + layer), preferred_element_type=F32
                )

        def pair_part(number, carry):
            work = ((0, (0, 1), (0, 1)), (1, (0, 1), (0, 1)), (2, (0,), (0,)))
            for buffer in (0, 1):
                tiles(*carry[buffer], work, buffer=buffer)
            for buffer in (0, 1):
                lead(carry[2 + buffer], buffer)
            return carry[2], carry[3], locate(lax.rem(2 * number + 4, 64)), locate(lax.rem(2 * number + 5, 64))

        def phase_part(phase, carry):

            @pl.when(phase == 1)
            def _():
                halo_cm.wait_recv()
                halo_cp.wait_recv()
                halo_a.start()

            @pl.when(phase == 2)
            def _():
                halo_a.wait_recv()

                def side(index):
                    for layer in range(3):
                        prepare_right(e, index, 5, layer)

                def front(index):
                    for layer in range(3):
                        prepare_right(e, 4, index, layer)

                loop(4, side)
                loop(6, front)

            @pl.when(phase == 3)
            def _():
                def give(index):
                    for layer in range(3):
                        net[e, 4, index, layer] = reduced(4, index, layer)

                loop(6, give)
                back_a.start()

            @pl.when(phase == 4)
            def _():
                back_a.wait_recv()
                for layer in range(3):
                    net[e, 0, 0, layer] = reduced(0, 0, layer) + in_a[e, 0, layer]

                def give(index):
                    for layer in range(3):
                        net[e, index, 5, layer] = reduced(index, 5, layer)

                loop(4, give)
                for layer in range(3):
                    net[e, 0, 5, layer] += in_a[e, 5, layer]
                back_cp.start()
                back_cm.start()

            start, stop = (pick(((1, x), (2, y), (3, z), (4, w)), v, phase) for x, y, z, w, v in zip(
                (0, 5), (5, 11), (11, 23), (23, 27), (27, 32)))
            return lax.fori_loop(start, stop, pair_part, carry)

        begin = tuple(locate(jnp.int32(number)) for number in range(4))
        lead(begin[0], 0)
        lead(begin[1], 1)
        lax.fori_loop(0, 5, phase_part, begin)

        back_cp.wait_recv()
        back_cm.wait_recv()

        def give_above(a):
            for c in range(4):
                net[e, a, c + 1, 2] = reduced(a, c + 1, 2)

        loop(4, give_above)
        for c in range(4):
            net[e, 0, c + 1, 2] += in_a[e, c + 1, 2]
        for a in range(4):
            net[e, a, 1, 2] += in_cp[e, a, 2]
        net[e, 0, 4, 2] += in_cm[e, 2]
        back_d.start()

        def collect(number):
            for a, c in ((number, c) for c in range(4)):
                index = a * 4 + c
                halves = [[], []]
                for layer in (0, 1):
                    sums = [acc_l[index, k, layer * W : layer * W + W] for k in range(4)]
                    low = lane_id < 64
                    for half, (x, y) in zip(halves, (sums[0:2], sums[2:4])):
                        both = jnp.where(low, x, y) + pltpu.roll(jnp.where(low, y, x), 64, 1)
                        top = both.astype(BF16)
                        half.append(jnp.concatenate([top, (both - top.astype(F32)).astype(BF16)], 1))
                left = None
                for number_of_half, half in enumerate(halves):
                    part = lax.dot_general(
                        picks[number_of_half], jnp.concatenate(half, 0), (((1,), (1,)), ((), ())),
                        preferred_element_type=F32,
                    )
                    left = part if left is None else left + part
                for layer in (0, 1):
                    own[a, c, layer] = left[0:8, layer * W : layer * W + W] + reduced(a, c + 1, layer)

        loop(4, collect)
        for c in range(4):
            for layer in (0, 1):
                own[0, c, layer] += in_a[e, c + 1, layer]
        for a in range(4):
            for layer in (0, 1):
                own[a, 0, layer] += in_cp[e, a, layer]
        for layer in (0, 1):
            own[0, 3, layer] += in_cm[e, layer]
        back_d.wait_recv()

        def settled(a, c, layer):
            state = raw[0, a, c + 1, layer]
            total = own[a, c, layer]
            if layer == 0:
                total = total + in_d[e, a, c] * mirror
            return state, total * (-KERNEL / state[7:8]) + gravity

        @pl.when(e == 0)
        def _():
            def half_way(a):
                keep = (row_id >= 3) & (row_id < 7)
                for c, layer in ((c, layer) for c in range(4) for layer in (0, 1)):
                    state, rate = settled(a, c, layer)
                    place = state + HALF * pltpu.roll(state, 5, 0)
                    raw[1, a, c + 1, layer] = jnp.where(
                        keep, state + HALF * rate, jnp.where(row_id < 3, place, state))

            loop(4, half_way)

        @pl.when(e == 1)
        def _():
            def finish(a):
                for c, layer in ((c, layer) for c in range(4) for layer in (0, 1)):
                    state, rate = settled(a, c, layer)
                    at = pl.ds(depth_of(layer), 1)
                    turn = jnp.where((row_id == 2) | (row_id == 5), sign, 1.0)
                    start = state * turn
                    start = jnp.where(row_id < 3, start + 0.5, start)
                    rate_g = rate * turn
                    corr = start + HALF * rate_g
                    place = start + HALF * pltpu.roll(corr, 5, 0)
                    new = jnp.where(row_id < 3, 2.0 * place - start, 2.0 * corr - start)
                    for k in range(7):
                        adv[k, a, c, at, :] = new[k : k + 1]
                    rates[0, a, c, at, :] = rate_g[6:7]
                    for k in range(3):
                        rates[k + 1, a, c, at, :] = rate_g[3 + k : 4 + k]

            loop(4, finish)

        for item in (halo_d, halo_cm, halo_cp, halo_a, back_a, back_cp, back_cm, back_d):
            item.wait_send()

    loop(2, evaluate)


def shards(counts, offsets, velocity, density, mass, pairs):
    vmem = pl.BlockSpec(memory_space=pltpu.VMEM)
    smem = pl.BlockSpec(memory_space=pltpu.SMEM)

    def body(*refs):
        step_kernel(counts, *refs)

    return pl.pallas_call(
        body,
        out_shape=(
            jax.ShapeDtypeStruct((4, 4, 4, 2, W), F32),
            jax.ShapeDtypeStruct((7, 4, 4, 2, W), F32),
        ),
        in_specs=[vmem, vmem, vmem, vmem, smem],
        out_specs=(vmem, vmem),
        scratch_shapes=[
            pltpu.VMEM((9, 80, 2 * W), BF16),
            pltpu.VMEM((9, 8, W), F32),
            pltpu.VMEM((W, 4 * W), BF16),
            pltpu.VMEM((2, 16, 2 * W), BF16),
            pltpu.VMEM((2, 5 * W, 2 * W), F32),
            pltpu.VMEM((2, 5, 6, 3, 8, W), F32),
            pltpu.VMEM((90, 32, 2 * W), BF16),
            pltpu.VMEM((90, 32, W), BF16),
            pltpu.VMEM((90, 8, W), F32),
            pltpu.VMEM((16, 2 * W, W), BF16),
            pltpu.VMEM((16, 6, 2 * W, W), F32),
            pltpu.VMEM((16, 4, 2 * W, W), F32),
            pltpu.VMEM((90, 4, 8, W), F32),
            pltpu.VMEM((2, 5, 6, 3, 8, W), F32),
            pltpu.VMEM((4, 4, 2, 8, W), F32),
            pltpu.VMEM((2, 6, 3, 8, W), F32),
            pltpu.VMEM((2, 4, 3, 8, W), F32),
            pltpu.VMEM((2, 3, 8, W), F32),
            pltpu.VMEM((2, 4, 4, 8, W), F32),
            pltpu.SemaphoreType.DMA((2, 8)),
            pltpu.SemaphoreType.DMA((2, 8)),
        ],
        compiler_params=pltpu.CompilerParams(
            collective_id=0, has_side_effects=True, vmem_limit_bytes=40 * 1024 * 1024
        ),
        name="sph_step",
    )(offsets, velocity, density, mass, pairs.reshape(-1))


def solution(mesh):
    counts = (mesh.shape["along"], mesh.shape["cross"])

    def run(*args):
        return shards(counts, *args)

    spec = P(None, "along", "cross", "depth", None)
    plain = P("along", "cross", "depth", None)
    return jax.shard_map(
        run,
        mesh=mesh,
        in_specs=(spec, spec, plain, plain, P(None, "along", "cross", "depth")),
        out_specs=(spec, spec),
        check_vma=False,
    )
```
